256 devices in a mesh: dp: 16 (over x, y), mp: 16 (over z, core).
Axes of the slice: x: 4, y: 4, z: 8, core: 2. Of those that a mesh axis runs over, the one named last changes fastest.
Arguments:
- pooled_in: bfloat16 [65536, 2048], P(('dp', 'mp')), may hold values from -24 to 24
- out_grad: bfloat16 [65536, 2048], P(('dp', 'mp')), may hold values from -6 to 6
- pooled_grad: bfloat16 [65536, 2048], P(('dp', 'mp')), may hold values from -6 to 6
- hot_ids: int32 [65536, 16], P(('dp', 'mp')), may hold values from 0 to 2047
- cold_owner: int32 [1048576, 1], P(('dp', 'mp')), may hold values from 0 to 255; in each aligned block of 4096 rows (0 to 4095, 4096 to 8191, ...) at most 32 rows name the same one
- cold_rows: int32 [65536, 16], P(('dp', 'mp')), may hold values from 0 to 4095
- mlp_weight: float32 [2048, 2048], P(('dp', 'mp')), may hold values from -0.125 to 0.125
- mlp_accum: float32 [2048, 2048], P(('dp', 'mp')), may hold values from 0.1 to 4
- hot_table: float32 [2048, 128], replicated, may hold values from -3 to 3
- hot_accum: float32 [2048], replicated, may hold values from 0.25 to 2048
- cold_table: float32 [1048576, 128], P(('dp', 'mp')), may hold values from -3 to 3
- cold_accum: float32 [1048576], P(('dp', 'mp')), may hold values from 0.1 to 4
Outputs:
- new_weight: float32 [2048, 2048], P(('dp', 'mp'))
- new_mlp_accum: float32 [2048, 2048], P(('dp', 'mp'))
- new_hot: float32 [2048, 128], replicated
- new_hot_accum: float32 [2048], replicated
- new_cold: float32 [1048576, 128], P(('dp', 'mp'))
- new_cold_accum: float32 [1048576], P(('dp', 'mp'))
The draws below stay inside these ranges and needn't reach their ends.
Inputs may be any that keep to these rules, and one draw needn't show every extreme that they name: `cold_owner`: among the rows of one device no owner is named by more than 32 rows; some owner is named by exactly 32.
All inputs are finite; a program needn't handle non-finite values.
Results may differ from the reference program's by a relative error of at most 0.0003.
Values may be sent and summed in bfloat16 or wider, within the bound.
A program may use at most 128 MiB of HBM per device.

```python
import math
import jax
import jax.numpy as jnp
import numpy as np
from jax import lax

EMB = 128
F = 16
HID = 2048
HOT = 2048
B_DEV = 256
ROWS_DEV = 4096
SAMPLES = 65536
ROWS = 1048576
CAP = 32
N_DP = 16
N_MP = 16


def plant(drawn, key, smallest, high):
    shape = drawn.shape
    index_at = [jax.random.randint(jax.random.fold_in(key, axis), (), 0, shape[axis]) for axis in range(len(shape))]
    drawn = drawn.at[tuple(index_at)].set(smallest)
    longest = shape.index(max(shape))
    index_at[longest] = (index_at[longest] + 1) % shape[longest]
    return drawn.at[tuple(index_at)].set(high)


def spiked(drawn, rng, source, target, parts, factor):
    owner, partner = [(jnp.arange(drawn.shape[position]) // (drawn.shape[position] // parts)).reshape([-1 if axis == position else 1 for axis in range(drawn.ndim)]) for position in (source, target)]
    chosen = jax.random.permutation(rng, parts)[partner]
    strong = (owner == chosen) | (owner == (partner + parts // 2) % parts)
    return jnp.where(strong, factor * drawn, drawn)


def levels(key, shape, split, smallest, high):
    level, own = 1.0, jax.random.fold_in(key, 6)
    for position, parts in split:
        draws = jnp.exp(jax.random.uniform(jax.random.fold_in(own, position), (parts,), jnp.float32, smallest / len(split), high / len(split)))
        level = level * jnp.repeat(draws, shape[position] // parts).reshape([-1 if axis == position else 1 for axis in range(len(shape))])
    return level


def rank_bounds(count, slope):
    loads = [(1 << 20) // math.isqrt(grade ** slope) + 1 for grade in range(1, count + 1)]
    scale = 1 + sum(loads) // (1 << 30)
    return np.cumsum(np.array([max(1, weight // scale) for weight in loads]))


def ranked_ids(key, extent, amount, skew):
    listing = rank_bounds(amount, skew)
    ticket = jax.random.randint(jax.random.fold_in(key, 1), extent, 0, int(listing[amount - 1]))
    standing = jnp.searchsorted(jnp.asarray(listing, jnp.int32), ticket, side="right")
    return jax.random.permutation(jax.random.fold_in(key, 2), amount)[standing].astype(jnp.int32)


def shared_out(key, own, number, rows, number_of, top, reach, slope):
    sequence = jax.random.permutation(key, number_of)
    packed, usual = shares(number_of, rows * top, reach, slope, True), shares(number_of, rows * top, reach, slope, False)
    places = jnp.arange(number_of)

    def named(sizes, offset_by):
        used = int((sizes > 0).sum())
        fixed = max(1, used // 4)
        shifted = fixed + (places - fixed + offset_by * (used - fixed)) % max(1, number_of - fixed)
        return jnp.zeros((number_of,), jnp.int32).at[sequence[jnp.where(places < fixed, places, shifted)]].set(jnp.asarray(sizes, jnp.int32))

    sizes = jnp.where(number % 4 == 0, named(packed, number // 4), named(usual, number - number // 4 - 1))
    mixed = jax.random.permutation(jax.random.fold_in(own, 3), number_of)
    giver, receiver = mixed[0:number_of // 2 * 2:2], mixed[1:number_of // 2 * 2:2]
    room = jnp.minimum(sizes[giver] - 1, reach - sizes[receiver]) // 2
    room = jnp.where((giver == sequence[0]) | (receiver == sequence[0]) | (sizes[receiver] == 0), 0, jnp.maximum(room, 0))
    shifted = jax.random.randint(jax.random.fold_in(own, 4), (number_of // 2,), 0, 1 << 20) % (room + 1)
    sizes = sizes.at[giver].add(-shifted).at[receiver].add(shifted)
    members = jnp.searchsorted(jnp.cumsum(sizes), jnp.arange(rows * top), side="right").astype(jnp.int32)
    listing = members.reshape(top, rows).T
    listing = listing[jax.random.permutation(jax.random.fold_in(own, 1), rows)]
    offset_by = jax.random.randint(jax.random.fold_in(own, 2), (rows, 1), 0, top)
    return jnp.take_along_axis(listing, (jnp.arange(top)[None, :] + offset_by) % top, axis=1)


def shares(count, total, most, lean, full):
    portions = [(1 << 20) // math.isqrt(standing ** lean) + 1 for standing in range(1, count + 1)]
    largest = most if full else min(most, max(-(-total // count), total * portions[0] // sum(portions)))
    least = 1 if total - largest >= count - 1 else 0
    given, rest = [largest] + [least] * (count - 1), total - largest - least * (count - 1)
    while rest > 0:
        movable = [i for i in range(1, count) if given[i] < largest] or [i for i in range(1, count) if given[i] < most]
        mass, budget = sum([portions[i] for i in movable]), rest
        for i in movable:
            extra = min(most - given[i], max(1, budget * portions[i] // mass), rest)
            given[i] = given[i] + extra
            rest = rest - extra
    return np.array(given)


def normal_values(own_key, extent, spread, reach, split=(), kind=jnp.bfloat16):
    factor_of = levels(own_key, extent, split, -0.22, 0.18) if split else 1.0
    drawn = jax.random.normal(own_key, extent, jnp.float32) * spread * factor_of
    return jnp.minimum(jnp.maximum(drawn, -reach), reach).astype(kind)


def noise_with(stream_key, shape, width, bound, shards, heavy, kind=jnp.bfloat16):
    result = width * jax.random.normal(stream_key, shape, jnp.float32)
    if shards:
        result = result * levels(stream_key, shape, shards, -0.22, 0.18)
    return jnp.clip(spiked(result, jax.random.fold_in(stream_key, 3), *heavy), -bound, bound).astype(kind)


def setup_inputs(seed: int = 0) -> dict:
    arg_keys = jax.random.split(jax.random.key(seed), 13)
    pooled_in = noise_with(arg_keys[0], (SAMPLES, HID), 1.0, 24.0, ((0, 256),), (0, 1, 256, 6.0))
    out_grad = normal_values(arg_keys[1], (SAMPLES, HID), 1.0, 6.0, ((0, 256),))
    pooled_grad = normal_values(arg_keys[2], (SAMPLES, HID), 1.0, 6.0, ((0, 256),))
    hot_ids = plant(ranked_ids(arg_keys[3], (SAMPLES, F), HOT, 2), jax.random.fold_in(arg_keys[3], 3), 0, HOT - 1).astype(jnp.int32)
    cold_owner_keys = jax.random.split(jax.random.fold_in(arg_keys[4], 1), (SAMPLES * F) // (B_DEV * F))
    cold_owner_turns = jax.random.permutation(jax.random.fold_in(arg_keys[4], 3), (SAMPLES * F) // (B_DEV * F))
    cold_owner = jax.vmap(lambda own, number: shared_out(jax.random.fold_in(arg_keys[4], 2), own, number, B_DEV * F, N_DP * N_MP, 1, CAP, 2))(cold_owner_keys, cold_owner_turns).reshape((SAMPLES * F, 1))
    cold_rows = plant(jax.random.randint(arg_keys[5], (SAMPLES, F), 0, ROWS_DEV), jax.random.fold_in(arg_keys[5], 1), 0, ROWS_DEV - 1).astype(jnp.int32)
    mlp_weight = normal_values(arg_keys[6], (HID, HID), HID ** -0.5, 0.125, ((0, 256),), jnp.float32)
    mlp_accum = jnp.clip(jnp.exp(math.log(4.0) - 3.6888794 * jax.random.uniform(arg_keys[7], (HID, HID), jnp.float32) ** levels(arg_keys[7], (HID, HID), ((0, 256),), -0.2, 0.2)), 0.1, 4.0)
    hot_table = normal_values(arg_keys[8], (HOT, EMB), 0.5, 3.0, (), jnp.float32)
    hot_accum = jnp.clip(jnp.exp(jax.random.uniform(arg_keys[9], (HOT,), jnp.float32, math.log(0.25), math.log(2048.0))), 0.25, 2048.0)
    cold_table = normal_values(arg_keys[10], (ROWS, EMB), 0.5, 3.0, ((0, 256),), jnp.float32)
    cold_accum = jnp.clip(jnp.exp(math.log(4.0) - 3.6888794 * jax.random.uniform(arg_keys[11], (ROWS,), jnp.float32) ** levels(arg_keys[11], (ROWS,), ((0, 256),), -0.2, 0.2)), 0.1, 4.0)
    return {"pooled_in": pooled_in, "out_grad": out_grad, "pooled_grad": pooled_grad, "hot_ids": hot_ids, "cold_owner": cold_owner, "cold_rows": cold_rows, "mlp_weight": mlp_weight, "mlp_accum": mlp_accum, "hot_table": hot_table, "hot_accum": hot_accum, "cold_table": cold_table, "cold_accum": cold_accum}


learn_rate = 0.1

def adagrad_rows(table, accum, grads):
    accum_new = accum + lax.optimization_barrier(jnp.mean(grads * grads, axis=1))
    return (table - learn_rate * grads / jnp.sqrt(accum_new)[:, None], accum_new)

def reference(pooled_in, out_grad, pooled_grad, hot_ids, cold_owner, cold_rows, mlp_weight, mlp_accum, hot_table, hot_accum, cold_table, cold_accum):
    weight_grad = jnp.dot(pooled_in.T, out_grad, preferred_element_type=jnp.float32) * SAMPLES ** (-0.5)
    new_mlp_accum = mlp_accum + weight_grad * weight_grad
    new_weight = mlp_weight - learn_rate * weight_grad / jnp.sqrt(new_mlp_accum)
    lookup_grad = pooled_grad.reshape(SAMPLES * F, EMB).astype(jnp.float32)
    hot_grad = jax.ops.segment_sum(lookup_grad, hot_ids.reshape(-1).astype(jnp.int32), num_segments=HOT)
    global_rows = (cold_owner[:, 0] * ROWS_DEV + cold_rows.reshape(-1)).astype(jnp.int32)
    cold_grad = jax.ops.segment_sum(lookup_grad, global_rows, num_segments=ROWS_DEV * N_DP * N_MP)
    new_hot, new_hot_accum = adagrad_rows(hot_table, hot_accum, hot_grad)
    new_cold, new_cold_accum = adagrad_rows(cold_table, cold_accum, cold_grad)
    return (new_weight, new_mlp_accum, new_hot, new_hot_accum, new_cold, new_cold_accum)
```

```python
import functools

import jax
import jax.numpy as jnp
from jax import lax
from jax.experimental import pallas as pl
from jax.experimental.pallas import tpu as pltpu
from jax.sharding import PartitionSpec as P

MESH = pl.DeviceIdType.MESH
RATE = 0.1
LANES = 128
F32 = jnp.float32
BF16 = jnp.bfloat16
I32 = jnp.int32
VMEM = pl.BlockSpec(memory_space=pltpu.VMEM)


def iota(shape, axis):
    return lax.broadcasted_iota(I32, shape, axis)


def onehot(rows, values):
    match = iota((rows, values.shape[1]), 0) == values
    return jnp.where(match, 1.0, 0.0).astype(BF16)


def dot(a, b):
    return lax.dot_general(a, b, (((1,), (0,)), ((), ())), preferred_element_type=F32)


def dot_t(a, b):
    return lax.dot_general(a, b, (((0,), (0,)), ((), ())), preferred_element_type=F32)


def adagrad_block(table, accum_row, grad):
    eye = iota((LANES, LANES), 0) == iota((LANES, LANES), 1)
    accum = jnp.sum(jnp.where(eye, accum_row, 0.0), axis=1, keepdims=True)
    new_accum = accum + jnp.sum(grad * grad, axis=1, keepdims=True) * (1.0 / LANES)
    new_table = table - grad * (RATE / jnp.sqrt(new_accum))
    new_row = jnp.sum(jnp.where(eye, new_accum, 0.0), axis=0, keepdims=True)
    return new_table, new_row


def bucket_kernel(cap, owner_ref, rows_ref, grad_ref, send_ref, ids_ref, rank_row, rhs, lhs):
    features, samples = owner_ref.shape
    devices = ids_ref.shape[0]
    earlier = jnp.where(
        iota((samples, samples), 0) < iota((samples, samples), 1), 1.0, 0.0
    ).astype(BF16)
    base = jnp.zeros((devices, 1), F32)
    for f in range(features):
        hot = onehot(devices, owner_ref[f : f + 1, :])
        hot32 = hot.astype(F32)
        before = dot(hot, earlier) + base
        rank_row[f : f + 1, :] = jnp.sum(hot32 * before, axis=0, keepdims=True)
        base = base + jnp.sum(hot32, axis=1, keepdims=True)
    rank_col = jnp.transpose(rank_row[...]).astype(I32)
    high = jnp.zeros((devices, LANES), F32)
    low = jnp.zeros((devices, LANES), F32)
    lane = iota((samples, LANES), 1)
    for f in range(features):
        rank = rank_col[:, f : f + 1]
        grad = grad_ref[:, f * LANES : (f + 1) * LANES]
        zero = jnp.zeros_like(grad)
        odd = jnp.broadcast_to(rank, (samples, LANES)) % 2 == 1
        rhs[f * samples : (f + 1) * samples, :LANES] = jnp.where(odd, zero, grad)
        rhs[f * samples : (f + 1) * samples, LANES:] = jnp.where(odd, grad, zero)
        row = rows_ref[:, f : f + 1]
        at = lane == rank
        hot = onehot(devices, owner_ref[f : f + 1, :])
        high += dot(hot, jnp.where(at, (row // 64 + 1).astype(F32), 0.0).astype(BF16))
        low += dot(hot, jnp.where(at, (row % 64).astype(F32), 0.0).astype(BF16))
    ids_ref[...] = (high * 64.0 + low - 64.0).astype(I32)
    slots = owner_ref[...] * (cap // 2) + rank_row[...].astype(I32) // 2
    step = samples

    def block(m, _):
        for f in range(features):
            lhs[:, f * samples : (f + 1) * samples] = onehot(step, slots[f : f + 1, :] - m * step)
        send_ref[pl.ds(m * step, step), :] = dot(lhs[...], rhs[...]).astype(BF16)
        return 0

    lax.fori_loop(0, send_ref.shape[0] // step, block, 0)


def hot_kernel(row_ref, col_ref, grad_ref, out_ref, rhs, lhs):
    features, samples = row_ref.shape
    half = out_ref.shape[0]
    for f in range(features):
        grad = grad_ref[:, f * LANES : (f + 1) * LANES]
        zero = jnp.zeros_like(grad)
        upper = jnp.broadcast_to(col_ref[:, f : f + 1], (samples, LANES)) >= half
        rhs[f * samples : (f + 1) * samples, :LANES] = jnp.where(upper, zero, grad)
        rhs[f * samples : (f + 1) * samples, LANES:] = jnp.where(upper, grad, zero)
    ids = row_ref[...]
    ids = jnp.where(ids >= half, ids - half, ids)
    step = samples

    def block(m, _):
        for f in range(features):
            lhs[:, f * samples : (f + 1) * samples] = onehot(step, ids[f : f + 1, :] - m * step)
        out_ref[pl.ds(m * step, step), :] = dot(lhs[...], rhs[...])
        return 0

    lax.fori_loop(0, half // step, block, 0)


def apply_kernel(row_ref, col_ref, grad_ref, table_ref, accum_ref, out_ref, new_accum_ref, rhs, lhs):
    slots = grad_ref.shape[0]
    half = table_ref.shape[0] // 2
    piece = 512
    for k in range(2):
        for i in range(0, slots, piece):
            grad = grad_ref[i : i + piece, k * LANES : (k + 1) * LANES]
            zero = jnp.zeros_like(grad)
            upper = jnp.broadcast_to(col_ref[i : i + piece, k : k + 1], (piece, LANES)) >= half
            at = k * slots + i
            rhs[at : at + piece, :LANES] = jnp.where(upper, zero, grad)
            rhs[at : at + piece, LANES:] = jnp.where(upper, grad, zero)
    step = 256

    def block(m, _):
        for k in range(2):
            for i in range(0, slots, piece):
                ids = row_ref[k : k + 1, i : i + piece]
                ids = jnp.where(ids >= half, ids - half, ids)
                at = k * slots + i
                lhs[:, at : at + piece] = onehot(step, ids - m * step)
        total = dot(lhs[...], rhs[...])
        for upper in range(2):
            for part in range(step // LANES):
                row = upper * half + m * step + part * LANES
                line = upper * (half // LANES) + m * (step // LANES) + part
                grad = total[part * LANES : (part + 1) * LANES, upper * LANES : (upper + 1) * LANES]
                table, accum = adagrad_block(
                    table_ref[pl.ds(row, LANES), :], accum_ref[pl.ds(line, 1), :], grad
                )
                out_ref[pl.ds(row, LANES), :] = table
                new_accum_ref[pl.ds(line, 1), :] = accum
        return 0

    lax.fori_loop(0, half // step, block, 0)


def reduce_kernel(
    nx, ny, nz, factor,
    x_ref, g_ref, hot_ref, w_ref, a_ref, ht_ref, ha_ref,
    nw_ref, na_ref, nh_ref, nha_ref,
    xp, gp, hp, prod, recv1, recv2, sums, recv3, total, last, hx, hy, hz, hsum, ss, rs,
):
    dp, mp = lax.axis_index("dp"), lax.axis_index("mp")
    x, y = lax.div(dp, ny), lax.rem(dp, ny)
    z, c = lax.div(mp, 2), lax.rem(mp, 2)

    def at_x(j):
        return (lax.rem(x + j, nx) * ny + y, mp)

    def at_y(j):
        return (x * ny + lax.rem(y + j, ny), mp)

    def at_z(j):
        return (dp, lax.rem(z + j, nz) * 2 + c)

    partner = (dp, z * 2 + 1 - c)
    barrier = pltpu.get_barrier_semaphore()
    peers = [partner]
    peers += [at_x(j) for j in range(1, nx)] + [at_y(j) for j in range(1, ny)]
    peers += [at_z(j) for j in range(1, nz)]
    for peer in peers:
        pl.semaphore_signal(barrier, inc=1, device_id=peer, device_id_type=MESH)
    pl.semaphore_wait(barrier, len(peers))

    copies = []

    def send(src, dst, device):
        k = len(copies)
        copy = pltpu.make_async_remote_copy(
            src_ref=src, dst_ref=dst, send_sem=ss.at[k], recv_sem=rs.at[k],
            device_id=device, device_id_type=MESH,
        )
        copy.start()
        copies.append(copy)
        return copy

    half = g_ref.shape[1] // 2
    quarter = half // 2
    rows = x_ref.shape[1]
    got_g = send(g_ref.at[:, pl.ds(pl.multiple_of((1 - c) * half, half), half)], gp, partner)
    got_x = send(x_ref, xp, partner)
    got_h = send(hot_ref.at[:, pl.ds(pl.multiple_of((1 - c) * LANES, LANES), LANES)], hp, partner)
    got_g.wait_recv()
    got_x.wait_recv()

    n = (nx, ny)
    chunk = rows // nx
    tile = rows // (nx * ny)
    here = (x, y)

    def compute(h, rel):
        dest = lax.rem(here[h] + rel, n[h])
        cols = pl.ds(pl.multiple_of(c * half + h * quarter, quarter), quarter)
        for t in range(chunk // tile):
            if h == 0:
                at = dest * chunk + t * tile
            else:
                at = t * (rows // nx) + dest * tile
            at = pl.ds(pl.multiple_of(at, LANES), tile)
            prod[h, rel, t * tile : (t + 1) * tile, :] = dot_t(x_ref[:, at], g_ref[:, cols]) + dot_t(
                xp[:, at], gp[:, h * quarter : (h + 1) * quarter]
            )

    def ring_far(part, buf, up, down, size):
        a, b = (0, size // 2), (size // 2, size // 2)
        return send(part(2, *a), buf.at[0], up), send(part(2, *b), buf.at[1], down)

    def ring_near(part, buf, up, down, size):
        a, b = (0, size // 2), (size // 2, size // 2)
        return send(part(1, *b), buf.at[2], up), send(part(3, *a), buf.at[3], down)

    def ring_join(part, buf, up, down, size, far):
        a, b = (0, size // 2), (size // 2, size // 2)
        far[0].wait_recv()
        ref = part(1, *a)
        ref[...] = ref[...] + buf[0]
        one = send(ref, buf.at[4], up)
        far[1].wait_recv()
        ref = part(3, *b)
        ref[...] = ref[...] + buf[1]
        return one, send(ref, buf.at[5], down)

    def ring_end(part, buf, size, near, join):
        a, b = (0, size // 2), (size // 2, size // 2)
        for copy in near + join:
            copy.wait_recv()
        ref = part(0, *a)
        ref[...] = ref[...] + buf[3] + buf[4]
        ref = part(0, *b)
        ref[...] = ref[...] + buf[2] + buf[5]

    def part1(h):
        return lambda rel, start, size: prod.at[h, rel, pl.ds(start, size)]

    def part2(h):
        def part(rel, start, size):
            dest = lax.rem(here[1 - h] + rel, n[1 - h])
            return prod.at[h, 0, pl.ds(pl.multiple_of(dest * tile + start, 8), size)]

        return part

    ends = ((at_x(1), at_x(nx - 1)), (at_y(1), at_y(ny - 1)))
    far, near, join = [], [], []
    for h in range(2):
        compute(h, 2)
        far.append(ring_far(part1(h), recv1.at[h], *ends[h], chunk))
    for h in range(2):
        compute(h, 1)
        compute(h, 3)
        near.append(ring_near(part1(h), recv1.at[h], *ends[h], chunk))

    hot_rows = hp.shape[0]
    mine = pl.ds(pl.multiple_of(c * LANES, LANES), LANES)
    got_h.wait_recv()
    hp[...] = hp[...] + hot_ref[:, mine]
    hrx, hry, hrz = hot_rows // nx, hot_rows // (nx * ny), hot_rows // (nx * ny * nz)
    hots = [
        send(hp.at[pl.ds(pl.multiple_of(lax.rem(x + j, nx) * hrx, 8), hrx)], hx.at[j - 1], at_x(j))
        for j in range(1, nx)
    ]
    for h in range(2):
        compute(h, 0)
    for copy in hots:
        copy.wait_recv()
    base_x = pl.multiple_of(x * hrx, 8)
    ref = hp.at[pl.ds(base_x, hrx)]
    ref[...] = ref[...] + hx[0] + hx[1] + hx[2]
    base_y = pl.multiple_of(base_x + y * hry, 8)
    hots = [
        send(hp.at[pl.ds(pl.multiple_of(base_x + lax.rem(y + j, ny) * hry, 8), hry)], hy.at[j - 1], at_y(j))
        for j in range(1, ny)
    ]
    for h in range(2):
        join.append(ring_join(part1(h), recv1.at[h], *ends[h], chunk, far[h]))
    for copy in hots:
        copy.wait_recv()
    ref = hp.at[pl.ds(base_y, hry)]
    ref[...] = ref[...] + hy[0] + hy[1] + hy[2]
    base_z = pl.multiple_of(base_y + z * hrz, 8)
    hots = [
        send(hp.at[pl.ds(pl.multiple_of(base_y + lax.rem(z + j, nz) * hrz, 8), hrz)], hz.at[j - 1], at_z(j))
        for j in range(1, nz)
    ]
    for copy in hots:
        copy.wait_recv()
    got = hp[pl.ds(base_z, hrz), :]
    for j in range(1, nz):
        got = got + hz[j - 1]
    base_c = pl.multiple_of(c * hot_rows, 8)
    own_z = pl.multiple_of(base_c + base_z, 8)
    hsum[pl.ds(own_z, hrz), :] = got
    own = hsum.at[pl.ds(own_z, hrz)]
    hots = [send(own, own, at_z(j)) for j in range(1, nz)]
    for copy in hots:
        copy.wait_recv()
    own = hsum.at[pl.ds(pl.multiple_of(base_c + base_y, 8), hry)]
    hots = [send(own, own, at_y(j)) for j in range(1, ny)]
    for copy in hots:
        copy.wait_recv()
    own = hsum.at[pl.ds(pl.multiple_of(base_c + base_x, 8), hrx)]
    hots = [send(own, own, at_x(j)) for j in range(1, nx)]
    for copy in hots:
        copy.wait_recv()
    own = hsum.at[pl.ds(base_c, hot_rows)]
    got_hot = send(own, own, partner)

    second = (ends[1], ends[0])
    far2, near2, join2 = [], [], []
    for h in range(2):
        ring_end(part1(h), recv1.at[h], chunk, near[h], join[h])
        far2.append(ring_far(part2(h), recv2.at[h], *second[h], tile))
        near2.append(ring_near(part2(h), recv2.at[h], *second[h], tile))

    got_hot.wait_recv()
    for i in range(hsum.shape[0] // LANES):
        at = slice(i * LANES, (i + 1) * LANES)
        table, accum = adagrad_block(ht_ref[at, :], ha_ref[i : i + 1, :], hsum[at, :])
        nh_ref[at, :] = table
        nha_ref[i : i + 1, :] = accum

    for h in range(2):
        join2.append(ring_join(part2(h), recv2.at[h], *second[h], tile, far2[h]))
    for h in range(2):
        ring_end(part2(h), recv2.at[h], tile, near2[h], join2[h])
        at = pl.multiple_of(here[1 - h] * tile, 8)
        sums[:, h * quarter : (h + 1) * quarter] = prod[h, 0, pl.ds(at, tile), :]
    band = tile // nz
    gots = [
        send(sums.at[pl.ds(pl.multiple_of(lax.rem(z + j, nz) * band, 8), band)], recv3.at[j - 1], at_z(j))
        for j in range(1, nz)
    ]
    value = sums[pl.ds(pl.multiple_of(z * band, 8), band), :]
    for j in range(1, nz):
        gots[j - 1].wait_recv()
        value = value + recv3[j - 1]
    total[...] = value
    out_rows = band // 2
    got = send(total.at[pl.ds(pl.multiple_of((1 - c) * out_rows, 8), out_rows)], last, partner)
    got.wait_recv()
    own = total[pl.ds(pl.multiple_of(c * out_rows, 8), out_rows), :]
    other = last[...]
    for side in range(2):
        cols = slice(side * half, (side + 1) * half)
        grad = jnp.where(c == side, own, other) * factor
        accum = a_ref[:, cols] + grad * grad
        na_ref[:, cols] = accum
        nw_ref[:, cols] = w_ref[:, cols] - RATE * grad / jnp.sqrt(accum)
    for copy in copies:
        copy.wait_send()


def shards(
    nx, ny, nz,
    pooled_in, out_grad, pooled_grad, hot_ids, cold_owner, cold_rows,
    mlp_weight, mlp_accum, hot_table, hot_accum, cold_table, cold_accum,
):
    devices = nx * ny * nz * 2
    samples, features = hot_ids.shape
    hid = pooled_in.shape[1]
    hot = hot_table.shape[0]
    rows = cold_table.shape[0]
    lookups = samples * features
    cap = 2 * lookups // devices
    slots = devices * cap // 2
    params = functools.partial(pltpu.CompilerParams, vmem_limit_bytes=48 << 20)

    owner_row = cold_owner.reshape(samples, features).T
    send_grad, ids = pl.pallas_call(
        functools.partial(bucket_kernel, cap),
        out_shape=(
            jax.ShapeDtypeStruct((slots, 2 * LANES), BF16),
            jax.ShapeDtypeStruct((devices, LANES), I32),
        ),
        in_specs=[VMEM] * 3,
        out_specs=(VMEM, VMEM),
        scratch_shapes=[
            pltpu.VMEM((features, samples), F32),
            pltpu.VMEM((lookups, 2 * LANES), BF16),
            pltpu.VMEM((samples, lookups), BF16),
        ],
        compiler_params=params(),
        name="bucket",
    )(owner_row, cold_rows, pooled_grad)
    got_ids = lax.all_to_all(ids[:, :cap], ("dp", "mp"), split_axis=0, concat_axis=0, tiled=True)
    got_grad = lax.all_to_all(
        send_grad.reshape(devices, cap // 2, 2 * LANES), ("dp", "mp"), split_axis=0, concat_axis=0, tiled=True
    ).reshape(slots, 2 * LANES)

    hot_part = pl.pallas_call(
        hot_kernel,
        out_shape=jax.ShapeDtypeStruct((hot // 2, 2 * LANES), F32),
        in_specs=[VMEM] * 3,
        out_specs=VMEM,
        scratch_shapes=[
            pltpu.VMEM((lookups, 2 * LANES), BF16),
            pltpu.VMEM((samples, lookups), BF16),
        ],
        compiler_params=params(),
        name="hot",
    )(hot_ids.T, hot_ids, pooled_grad)

    quarter = hid // 4
    chunk, tile = hid // nx, hid // (nx * ny)
    band = tile // nz
    half_hot = hot // 2
    hrx, hry, hrz = half_hot // nx, half_hot // (nx * ny), half_hot // (nx * ny * nz)
    n_copies = 3 + 2 * 6 * 2 + (nz - 1) + 1 + 2 * (nx - 1 + ny - 1 + nz - 1) + 1
    new_weight, new_mlp_accum, new_hot, new_hot_accum = pl.pallas_call(
        functools.partial(reduce_kernel, nx, ny, nz, float(samples * devices) ** (-0.5)),
        out_shape=(
            jax.ShapeDtypeStruct(mlp_weight.shape, F32),
            jax.ShapeDtypeStruct(mlp_accum.shape, F32),
            jax.ShapeDtypeStruct(hot_table.shape, F32),
            jax.ShapeDtypeStruct((hot // LANES, LANES), F32),
        ),
        in_specs=[VMEM] * 7,
        out_specs=(VMEM,) * 4,
        scratch_shapes=[
            pltpu.VMEM((samples, hid), BF16),
            pltpu.VMEM((samples, hid // 2), BF16),
            pltpu.VMEM((half_hot, LANES), F32),
            pltpu.VMEM((2, 4, chunk, quarter), F32),
            pltpu.VMEM((2, 6, chunk // 2, quarter), F32),
            pltpu.VMEM((2, 6, tile // 2, quarter), F32),
            pltpu.VMEM((tile, hid // 2), F32),
            pltpu.VMEM((nz - 1, band, hid // 2), F32),
            pltpu.VMEM((band, hid // 2), F32),
            pltpu.VMEM((band // 2, hid // 2), F32),
            pltpu.VMEM((nx - 1, hrx, LANES), F32),
            pltpu.VMEM((ny - 1, hry, LANES), F32),
            pltpu.VMEM((nz - 1, hrz, LANES), F32),
            pltpu.VMEM((hot, LANES), F32),
            pltpu.SemaphoreType.DMA((n_copies,)),
            pltpu.SemaphoreType.DMA((n_copies,)),
        ],
        compiler_params=params(collective_id=0, has_side_effects=True),
        name="reduce",
    )(
        pooled_in, out_grad, hot_part, mlp_weight, mlp_accum, hot_table,
        hot_accum.reshape(hot // LANES, LANES),
    )

    id_col = got_ids.reshape(slots, 2)
    new_cold, new_cold_accum = pl.pallas_call(
        apply_kernel,
        out_shape=(
            jax.ShapeDtypeStruct(cold_table.shape, F32),
            jax.ShapeDtypeStruct((rows // LANES, LANES), F32),
        ),
        in_specs=[VMEM] * 5,
        out_specs=(VMEM, VMEM),
        scratch_shapes=[
            pltpu.VMEM((2 * slots, 2 * LANES), BF16),
            pltpu.VMEM((256, 2 * slots), BF16),
        ],
        compiler_params=params(),
        name="apply",
    )(id_col.T, id_col, got_grad, cold_table, cold_accum.reshape(rows // LANES, LANES))
    return (
        new_weight,
        new_mlp_accum,
        new_hot,
        new_hot_accum.reshape(hot),
        new_cold,
        new_cold_accum.reshape(rows),
    )


def solution(mesh):
    split = P(("dp", "mp"), None)
    nx = ny = 4
    nz = mesh.shape["mp"] // 2
    return jax.shard_map(
        functools.partial(shards, nx, ny, nz),
        mesh=mesh,
        in_specs=(split,) * 8 + (P(), P(), split, P(("dp", "mp"))),
        out_specs=(split, split, P(), P(), split, P(("dp", "mp"))),
        check_vma=False,
    )
```

```python
import functools

import jax
import jax.numpy as jnp
from jax import lax
from jax.experimental import pallas as pl
from jax.experimental.pallas import tpu as pltpu
from jax.sharding import PartitionSpec as P

MESH = pl.DeviceIdType.MESH
RATE = 0.1
LANES = 128
F32 = jnp.float32
BF16 = jnp.bfloat16
I32 = jnp.int32
VMEM = pl.BlockSpec(memory_space=pltpu.VMEM)


def iota(shape, axis):
    return lax.broadcasted_iota(I32, shape, axis)


def onehot(rows, values):
    match = iota((rows, values.shape[1]), 0) == values
    return jnp.where(match, 1.0, 0.0).astype(BF16)


def dot(a, b):
    return lax.dot_general(a, b, (((1,), (0,)), ((), ())), preferred_element_type=F32)


def dot_t(a, b):
    return lax.dot_general(a, b, (((0,), (0,)), ((), ())), preferred_element_type=F32)


def adagrad_block(table, accum_row, grad):
    eye = iota((LANES, LANES), 0) == iota((LANES, LANES), 1)
    accum = jnp.sum(jnp.where(eye, accum_row, 0.0), axis=1, keepdims=True)
    new_accum = accum + jnp.sum(grad * grad, axis=1, keepdims=True) * (1.0 / LANES)
    new_table = table - grad * (RATE / jnp.sqrt(new_accum))
    new_row = jnp.sum(jnp.where(eye, new_accum, 0.0), axis=0, keepdims=True)
    return new_table, new_row


def dot_nt(a, b):
    return lax.dot_general(a, b, (((1,), (1,)), ((), ())), preferred_element_type=F32)


def split_columns(rhs, at, grad, upper):
    zero = jnp.zeros_like(grad)
    rows = grad.shape[0]
    rhs[at : at + rows, :LANES] = jnp.where(upper, zero, grad)
    rhs[at : at + rows, LANES:] = jnp.where(upper, grad, zero)


def step_kernel(
    nx, ny, nz, cap, factor,
    x_ref, g_ref, pg_ref, hid_ref, own_ref, row_ref, w_ref, a_ref, ht_ref, ha_ref, ct_ref, ca_ref,
    nw_ref, na_ref, nh_ref, nha_ref, nc_ref, nca_ref,
    xp, gp, prod, recv1, recv2, sums, recv3, total, last,
    hpart, hp, hx, hy, hz, hsum,
    rank_row, own_row, rhs, lhs, send_buf, mid, fin, idsend, idmid, idout, idfin, idrow, ids, arhs, alhs, cold,
    ss, rs, s1, r1, s2, r2, t1, q1, t2, q2,
):
    samples, features = hid_ref.shape
    n_dp, n_mp = nx * ny, nz * 2
    devices = n_dp * n_mp
    deep = cap // 2
    dp, mp = lax.axis_index("dp"), lax.axis_index("mp")
    x, y = lax.div(dp, ny), lax.rem(dp, ny)
    z, c = lax.div(mp, 2), lax.rem(mp, 2)

    def at_x(j):
        return (lax.rem(x + j, nx) * ny + y, mp)

    def at_y(j):
        return (x * ny + lax.rem(y + j, ny), mp)

    def at_z(j):
        return (dp, lax.rem(z + j, nz) * 2 + c)

    def at_dp(i):
        return lax.rem(x + lax.div(i, ny), nx) * ny + lax.rem(y + lax.rem(i, ny), ny)

    mid_z = nz // 2

    def at_mp(p):
        pz, pc = lax.div(p, 2), lax.rem(p, 2)
        jz = jnp.where(lax.rem(pz, 2) == 1, mid_z - lax.div(pz + 1, 2), mid_z + lax.div(pz, 2))
        return lax.rem(z + jz, nz) * 2 + lax.rem(c + pc, 2)

    here_slot = n_mp - 2
    partner = (dp, z * 2 + 1 - c)
    barrier = pltpu.get_barrier_semaphore()

    def greet_dp(i, _):
        pl.semaphore_signal(barrier, inc=1, device_id=(at_dp(i), mp), device_id_type=MESH)
        return 0

    def greet_mp(j, _):
        pl.semaphore_signal(
            barrier, inc=1, device_id=(dp, lax.rem(mp + j, n_mp)), device_id_type=MESH
        )
        return 0

    lax.fori_loop(1, n_dp, greet_dp, 0)
    lax.fori_loop(1, n_mp, greet_mp, 0)

    line = LANES // features
    spread = jnp.concatenate(
        [
            jnp.broadcast_to(own_ref[:, r * LANES : (r + 1) * LANES], (line, LANES))
            for r in range(own_ref.shape[1] // LANES)
        ],
        axis=0,
    )
    keep = iota((samples, LANES), 1) // features == iota((samples, LANES), 0) % line
    pick = jnp.where(iota((features, LANES), 1) % features == iota((features, LANES), 0), 1.0, 0.0)
    owner = dot_nt(pick.astype(BF16), jnp.where(keep, spread, 0).astype(F32).astype(BF16)).astype(I32)
    to_mp = owner % n_mp
    jz = (to_mp // 2 - z + nz) % nz
    pz = jnp.where(jz > mid_z, 2 * (jz - mid_z), jnp.maximum(2 * (mid_z - jz) - 1, 0))
    place = (pz * 2 + (to_mp + c) % 2) * n_dp + owner // n_mp
    own_row[...] = place
    earlier = jnp.where(
        iota((samples, samples), 0) < iota((samples, samples), 1), 1.0, 0.0
    ).astype(BF16)
    base = jnp.zeros((devices, 1), F32)
    for f in range(features):
        hot = onehot(devices, own_row[f : f + 1, :])
        hot32 = hot.astype(F32)
        before = dot(hot, earlier) + base
        rank_row[f : f + 1, :] = jnp.sum(hot32 * before, axis=0, keepdims=True)
        base = base + jnp.sum(hot32, axis=1, keepdims=True)

    pl.semaphore_wait(barrier, n_dp + n_mp - 2)

    copies = []

    def send(src, dst, device):
        k = len(copies)
        copy = pltpu.make_async_remote_copy(
            src_ref=src, dst_ref=dst, send_sem=ss.at[k], recv_sem=rs.at[k],
            device_id=device, device_id_type=MESH,
        )
        copy.start()
        copies.append(copy)
        return copy

    half = g_ref.shape[1] // 2
    quarter = half // 2
    rows = x_ref.shape[1]
    got_g = send(g_ref.at[:, pl.ds(pl.multiple_of((1 - c) * half, half), half)], gp, partner)
    got_x = send(x_ref, xp, partner)

    rank_col = jnp.transpose(rank_row[...]).astype(I32)
    lane = iota((samples, LANES), 1)
    numbers = jnp.zeros((devices, LANES), F32)
    for f in range(features):
        rank = jnp.broadcast_to(rank_col[:, f : f + 1], (samples, LANES))
        grad = pg_ref[:, f * LANES : (f + 1) * LANES]
        split_columns(rhs, f * samples, grad, rank % 2 == 1)
        row = jnp.broadcast_to(row_ref[:, f : f + 1], (samples, LANES))
        spot = (rank % 2) * deep + rank // 2
        digit = jnp.where(lane < cap, row // 64 + 1, row % 64)
        digit = jnp.where((lane % cap == spot) & (lane < 2 * cap), digit, 0).astype(F32).astype(BF16)
        numbers += dot(onehot(devices, own_row[f : f + 1, :]), digit)
    idsend[...] = numbers
    slots = own_row[...] * deep + rank_row[...].astype(I32) // 2
    own_row[...] = slots

    got_g.wait_recv()
    got_x.wait_recv()

    n = (nx, ny)
    chunk = rows // nx
    tile = rows // (nx * ny)
    here = (x, y)

    def compute(h, rel):
        dest = lax.rem(here[h] + rel, n[h])
        cols = pl.ds(pl.multiple_of(c * half + h * quarter, quarter), quarter)
        for t in range(chunk // tile):
            if h == 0:
                at = dest * chunk + t * tile
            else:
                at = t * (rows // nx) + dest * tile
            at = pl.ds(pl.multiple_of(at, LANES), tile)
            prod[h, rel, t * tile : (t + 1) * tile, :] = dot_t(x_ref[:, at], g_ref[:, cols]) + dot_t(
                xp[:, at], gp[:, h * quarter : (h + 1) * quarter]
            )

    def ring_far(part, buf, up, down, size):
        a, b = (0, size // 2), (size // 2, size // 2)
        return send(part(2, *a), buf.at[0], up), send(part(2, *b), buf.at[1], down)

    def ring_near(part, buf, up, down, size):
        a, b = (0, size // 2), (size // 2, size // 2)
        return send(part(1, *b), buf.at[2], up), send(part(3, *a), buf.at[3], down)

    def ring_join(part, buf, up, down, size, far):
        a, b = (0, size // 2), (size // 2, size // 2)
        far[0].wait_recv()
        ref = part(1, *a)
        ref[...] = ref[...] + buf[0]
        one = send(ref, buf.at[4], up)
        far[1].wait_recv()
        ref = part(3, *b)
        ref[...] = ref[...] + buf[1]
        return one, send(ref, buf.at[5], down)

    def ring_end(part, buf, size, near, join):
        a, b = (0, size // 2), (size // 2, size // 2)
        for copy in near + join:
            copy.wait_recv()
        ref = part(0, *a)
        ref[...] = ref[...] + buf[3] + buf[4]
        ref = part(0, *b)
        ref[...] = ref[...] + buf[2] + buf[5]

    def part1(h):
        return lambda rel, start, size: prod.at[h, rel, pl.ds(start, size)]

    def part2(h):
        def part(rel, start, size):
            dest = lax.rem(here[1 - h] + rel, n[1 - h])
            return prod.at[h, 0, pl.ds(pl.multiple_of(dest * tile + start, 8), size)]

        return part

    ends = ((at_x(1), at_x(nx - 1)), (at_y(1), at_y(ny - 1)))
    second = (ends[1], ends[0])
    far, near, join, far2, near2, join2 = [], [], [], [], [], []
    for h in range(2):
        compute(h, 2)
        far.append(ring_far(part1(h), recv1.at[h], *ends[h], chunk))
    for h in range(2):
        compute(h, 1)
        compute(h, 3)
        near.append(ring_near(part1(h), recv1.at[h], *ends[h], chunk))

    def hop(src, dst, send_sem, recv_sem, device):
        return pltpu.make_async_remote_copy(
            src_ref=src, dst_ref=dst, send_sem=send_sem, recv_sem=recv_sem,
            device_id=device, device_id_type=MESH,
        )

    def ids_one(p):
        at = pl.ds(pl.multiple_of(p * n_dp, 8), n_dp)
        return hop(idsend.at[at], idmid.at[p], t1.at[p], q1.at[p], (dp, at_mp(p)))

    def cold_one(p):
        return hop(send_buf.at[p], mid.at[p], s1.at[p], r1.at[p], (dp, at_mp(p)))

    def ids_two(i):
        to = at_dp(i)
        return hop(idout.at[to], idfin.at[i], t2.at[i], q2.at[i], (to, mp))

    groups = 4
    each = n_mp // groups

    def cold_two(g, i):
        to = at_dp(i)
        at = pl.ds(g * each, each)
        return hop(mid.at[at, to], fin.at[i, at], s2.at[g, i], r2.at[g, i], (to, mp))

    def every_mp(act):
        def body(p, _):
            @pl.when(p != here_slot)
            def _():
                act(p)

            return 0

        lax.fori_loop(0, n_mp, body, 0)

    def every_dp(act):
        def body(i, _):
            act(i)
            return 0

        lax.fori_loop(1, n_dp, body, 0)

    every_mp(lambda p: ids_one(p).start())

    def bucket(p, _):
        for f in range(features):
            lhs[:, f * samples : (f + 1) * samples] = onehot(
                n_dp * deep, own_row[f : f + 1, :] - p * (n_dp * deep)
            )
        block = dot(lhs[...], rhs[...]).astype(BF16)
        send_buf[p] = block.reshape(n_dp, deep, 2 * LANES)

        @pl.when(p != here_slot)
        def _():
            cold_one(p).start()

        return 0

    lax.fori_loop(0, n_mp, bucket, 0)
    mid[here_slot] = send_buf[here_slot]
    idmid[here_slot] = idsend[here_slot * n_dp : (here_slot + 1) * n_dp, :]

    for h in range(2):
        compute(h, 0)
    for h in range(2):
        join.append(ring_join(part1(h), recv1.at[h], *ends[h], chunk, far[h]))

    hot_rows = hp.shape[0]
    hot_ids = hid_ref[...]
    hot_row = jnp.transpose(hot_ids.astype(F32)).astype(I32)
    hot_row = jnp.where(hot_row >= hot_rows, hot_row - hot_rows, hot_row)
    own_row[...] = hot_row
    for f in range(features):
        upper = jnp.broadcast_to(hot_ids[:, f : f + 1], (samples, LANES)) >= hot_rows
        split_columns(rhs, f * samples, pg_ref[:, f * LANES : (f + 1) * LANES], upper)

    def hot_block(m, _):
        for f in range(features):
            lhs[:, f * samples : (f + 1) * samples] = onehot(samples, own_row[f : f + 1, :] - m * samples)
        hpart[pl.ds(pl.multiple_of(m * samples, 8), samples), :] = dot(lhs[...], rhs[...])
        return 0

    lax.fori_loop(0, hot_rows // samples, hot_block, 0)
    got_h = send(hpart.at[:, pl.ds(pl.multiple_of((1 - c) * LANES, LANES), LANES)], hp, partner)
    mine = pl.ds(pl.multiple_of(c * LANES, LANES), LANES)

    every_mp(lambda p: ids_one(p).wait_recv())
    for d in range(n_dp):
        idout[d] = jnp.concatenate([idmid[p, d : d + 1, :] for p in range(n_mp)], axis=0)
    every_dp(lambda i: ids_two(i).start())

    def forward(g):
        for p in range(g * each, (g + 1) * each):
            if p != here_slot:
                cold_one(p).wait_recv()
        every_dp(lambda i: cold_two(g, i).start())
        fin[0, g * each : (g + 1) * each] = mid[g * each : (g + 1) * each, dp]

    forward(0)

    hrx, hry, hrz = hot_rows // nx, hot_rows // (nx * ny), hot_rows // (nx * ny * nz)
    base_x = pl.multiple_of(x * hrx, 8)
    base_y = pl.multiple_of(base_x + y * hry, 8)
    base_z = pl.multiple_of(base_y + z * hrz, 8)
    base_c = pl.multiple_of(c * hot_rows, 8)
    own_z = pl.multiple_of(base_c + base_z, 8)
    got_h.wait_recv()
    hp[...] = hp[...] + hpart[:, mine]
    hots = [
        send(hp.at[pl.ds(pl.multiple_of(lax.rem(x + j, nx) * hrx, 8), hrx)], hx.at[j - 1], at_x(j))
        for j in range(1, nx)
    ]

    every_dp(lambda i: ids_two(i).wait_recv())
    idfin[0] = idout[dp]
    for g in range(groups):
        for i in range(n_dp):
            at = (g * n_dp + i) * each
            idrow[at : at + each, :] = idfin[i, g * each : (g + 1) * each, :]
    digits = idrow[...].astype(BF16)
    at_lane, at_digit = iota((LANES, 2 * LANES), 1), iota((LANES, 2 * LANES), 0)
    want = (at_lane // LANES) * deep + at_lane % deep
    high = dot(digits, jnp.where(at_digit == want, 1.0, 0.0).astype(BF16))
    low = dot(digits, jnp.where(at_digit == want + cap, 1.0, 0.0).astype(BF16))
    numbers = high * 64.0 + low - 64.0
    band8 = LANES // deep
    keep = (iota(numbers.shape, 1) % LANES) // deep == iota(numbers.shape, 0) % band8
    numbers = jnp.where(keep, numbers, 0.0)
    numbers = jnp.sum(numbers.reshape(devices // band8, band8, 2 * LANES), axis=1)
    ids[...] = numbers.astype(I32)

    forward(1)
    for copy in hots:
        copy.wait_recv()
    ref = hp.at[pl.ds(base_x, hrx)]
    ref[...] = ref[...] + hx[0] + hx[1] + hx[2]
    hots = [
        send(hp.at[pl.ds(pl.multiple_of(base_x + lax.rem(y + j, ny) * hry, 8), hry)], hy.at[j - 1], at_y(j))
        for j in range(1, ny)
    ]

    for h in range(2):
        ring_end(part1(h), recv1.at[h], chunk, near[h], join[h])
        far2.append(ring_far(part2(h), recv2.at[h], *second[h], tile))
        near2.append(ring_near(part2(h), recv2.at[h], *second[h], tile))

    for copy in hots:
        copy.wait_recv()
    ref = hp.at[pl.ds(base_y, hry)]
    ref[...] = ref[...] + hy[0] + hy[1] + hy[2]
    hots = [
        send(hp.at[pl.ds(pl.multiple_of(base_y + lax.rem(z + j, nz) * hrz, 8), hrz)], hz.at[j - 1], at_z(j))
        for j in range(1, nz)
    ]

    forward(2)

    cold_half = cold.shape[0]
    per = n_dp * each * deep
    pieces = per // LANES
    eye = iota((LANES, LANES), 0) == iota((LANES, LANES), 1)
    ones = jnp.ones((LANES, LANES), BF16)
    step = 256

    def arrived(g):
        every_dp(lambda i: cold_two(g, i).wait_recv())
        pair = LANES // (each * deep)
        for q in range(pieces):
            grads = fin[q * pair : (q + 1) * pair, g * each : (g + 1) * each].reshape(LANES, 2 * LANES)
            for k in range(2):
                number = ids[g * pieces + q : g * pieces + q + 1, k * LANES : (k + 1) * LANES]
                upper = jnp.where(number >= cold_half, 1.0, 0.0)
                column = dot(jnp.where(eye, upper, 0.0).astype(BF16), ones)
                split_columns(arhs, k * per + q * LANES, grads[:, k * LANES : (k + 1) * LANES], column > 0.5)

    def summed(g, m):
        for q in range(pieces):
            for k in range(2):
                number = ids[g * pieces + q : g * pieces + q + 1, k * LANES : (k + 1) * LANES]
                number = jnp.where(number >= cold_half, number - cold_half, number)
                at = k * per + q * LANES
                alhs[:, at : at + LANES] = onehot(step, number - m * step)
        return dot(alhs[...], arhs[...])

    def gather(g):
        arrived(g)

        def block(m, _):
            at = pl.ds(pl.multiple_of(m * step, 8), step)
            if g == 0:
                cold[at, :] = summed(g, m)
            else:
                cold[at, :] = cold[at, :] + summed(g, m)
            return 0

        lax.fori_loop(0, cold_half // step, block, 0)

    gather(0)

    for copy in hots:
        copy.wait_recv()
    got = hp[pl.ds(base_z, hrz), :]
    for j in range(1, nz):
        got = got + hz[j - 1]
    hsum[pl.ds(own_z, hrz), :] = got
    own = hsum.at[pl.ds(own_z, hrz)]
    hots = [send(own, own, at_z(j)) for j in range(1, nz)]

    for h in range(2):
        join2.append(ring_join(part2(h), recv2.at[h], *second[h], tile, far2[h]))
    forward(3)

    for copy in hots:
        copy.wait_recv()
    own = hsum.at[pl.ds(pl.multiple_of(base_c + base_y, 8), hry)]
    hots = [send(own, own, at_y(j)) for j in range(1, ny)]

    for h in range(2):
        ring_end(part2(h), recv2.at[h], tile, near2[h], join2[h])
        at = pl.multiple_of(here[1 - h] * tile, 8)
        sums[:, h * quarter : (h + 1) * quarter] = prod[h, 0, pl.ds(at, tile), :]
    band = tile // nz
    gots = [
        send(sums.at[pl.ds(pl.multiple_of(lax.rem(z + j, nz) * band, 8), band)], recv3.at[j - 1], at_z(j))
        for j in range(1, nz)
    ]

    gather(1)

    for copy in hots:
        copy.wait_recv()
    own = hsum.at[pl.ds(pl.multiple_of(base_c + base_x, 8), hrx)]
    hots = [send(own, own, at_x(j)) for j in range(1, nx)]

    gather(2)

    for copy in hots:
        copy.wait_recv()
    own = hsum.at[pl.ds(base_c, hot_rows)]
    got_hot = send(own, own, partner)

    value = sums[pl.ds(pl.multiple_of(z * band, 8), band), :]
    for j in range(1, nz):
        gots[j - 1].wait_recv()
        value = value + recv3[j - 1]
    total[...] = value
    out_rows = band // 2
    got = send(total.at[pl.ds(pl.multiple_of((1 - c) * out_rows, 8), out_rows)], last, partner)

    got_hot.wait_recv()
    for i in range(hsum.shape[0] // LANES):
        at = slice(i * LANES, (i + 1) * LANES)
        table, accum = adagrad_block(ht_ref[at, :], ha_ref[i : i + 1, :], hsum[at, :])
        nh_ref[at, :] = table
        nha_ref[i : i + 1, :] = accum

    got.wait_recv()
    own = total[pl.ds(pl.multiple_of(c * out_rows, 8), out_rows), :]
    other = last[...]
    for side in range(2):
        cols = slice(side * half, (side + 1) * half)
        grad = jnp.where(c == side, own, other) * factor
        accum = a_ref[:, cols] + grad * grad
        na_ref[:, cols] = accum
        nw_ref[:, cols] = w_ref[:, cols] - RATE * grad / jnp.sqrt(accum)

    g_last = groups - 1
    arrived(g_last)

    def finish(m, _):
        grads = summed(g_last, m) + cold[pl.ds(pl.multiple_of(m * step, 8), step), :]
        for upper in range(2):
            for part in range(step // LANES):
                row = pl.multiple_of(upper * cold_half + m * step + part * LANES, LANES)
                line = upper * (cold_half // LANES) + m * (step // LANES) + part
                grad = grads[part * LANES : (part + 1) * LANES, upper * LANES : (upper + 1) * LANES]
                table, accum = adagrad_block(
                    ct_ref[pl.ds(row, LANES), :], ca_ref[pl.ds(line, 1), :], grad
                )
                nc_ref[pl.ds(row, LANES), :] = table
                nca_ref[pl.ds(line, 1), :] = accum
        return 0

    lax.fori_loop(0, cold_half // step, finish, 0)

    for copy in copies:
        copy.wait_send()
    every_mp(lambda p: ids_one(p).wait_send())
    every_mp(lambda p: cold_one(p).wait_send())
    every_dp(lambda i: ids_two(i).wait_send())
    for g in range(groups):
        every_dp(lambda i: cold_two(g, i).wait_send())


def shards(
    nx, ny, nz,
    pooled_in, out_grad, pooled_grad, hot_ids, cold_owner, cold_rows,
    mlp_weight, mlp_accum, hot_table, hot_accum, cold_table, cold_accum,
):
    n_dp, n_mp = nx * ny, nz * 2
    devices = n_dp * n_mp
    samples, features = hot_ids.shape
    hid = pooled_in.shape[1]
    hot = hot_table.shape[0]
    rows = cold_table.shape[0]
    lookups = samples * features
    cap = 2 * lookups // devices
    deep = cap // 2
    group_slots = 2 * (n_dp * (n_mp // 4) * deep)
    quarter = hid // 4
    chunk, tile = hid // nx, hid // (nx * ny)
    band = tile // nz
    half_hot = hot // 2
    hrx, hry, hrz = half_hot // nx, half_hot // (nx * ny), half_hot // (nx * ny * nz)
    n_copies = 3 + 2 * 6 * 2 + (nz - 1) + 1 + 2 * (nx - 1 + ny - 1 + nz - 1) + 1
    dma = pltpu.SemaphoreType.DMA
    outs = pl.pallas_call(
        functools.partial(step_kernel, nx, ny, nz, cap, float(samples * devices) ** (-0.5)),
        out_shape=(
            jax.ShapeDtypeStruct(mlp_weight.shape, F32),
            jax.ShapeDtypeStruct(mlp_accum.shape, F32),
            jax.ShapeDtypeStruct(hot_table.shape, F32),
            jax.ShapeDtypeStruct((hot // LANES, LANES), F32),
            jax.ShapeDtypeStruct(cold_table.shape, F32),
            jax.ShapeDtypeStruct((rows // LANES, LANES), F32),
        ),
        in_specs=[VMEM] * 12,
        out_specs=(VMEM,) * 6,
        scratch_shapes=[
            pltpu.VMEM((samples, hid), BF16),
            pltpu.VMEM((samples, hid // 2), BF16),
            pltpu.VMEM((2, 4, chunk, quarter), F32),
            pltpu.VMEM((2, 6, chunk // 2, quarter), F32),
            pltpu.VMEM((2, 6, tile // 2, quarter), F32),
            pltpu.VMEM((tile, hid // 2), F32),
            pltpu.VMEM((nz - 1, band, hid // 2), F32),
            pltpu.VMEM((band, hid // 2), F32),
            pltpu.VMEM((band // 2, hid // 2), F32),
            pltpu.VMEM((half_hot, 2 * LANES), F32),
            pltpu.VMEM((half_hot, LANES), F32),
            pltpu.VMEM((nx - 1, hrx, LANES), F32),
            pltpu.VMEM((ny - 1, hry, LANES), F32),
            pltpu.VMEM((nz - 1, hrz, LANES), F32),
            pltpu.VMEM((hot, LANES), F32),
            pltpu.VMEM((features, samples), F32),
            pltpu.VMEM((features, samples), I32),
            pltpu.VMEM((lookups, 2 * LANES), BF16),
            pltpu.VMEM((samples, lookups), BF16),
            pltpu.VMEM((n_mp, n_dp, deep, 2 * LANES), BF16),
            pltpu.VMEM((n_mp, n_dp, deep, 2 * LANES), BF16),
            pltpu.VMEM((n_dp, n_mp, deep, 2 * LANES), BF16),
            pltpu.VMEM((devices, LANES), F32),
            pltpu.VMEM((n_mp, n_dp, LANES), F32),
            pltpu.VMEM((n_dp, n_mp, LANES), F32),
            pltpu.VMEM((n_dp, n_mp, LANES), F32),
            pltpu.VMEM((devices, LANES), F32),
            pltpu.VMEM((devices * deep // LANES, 2 * LANES), I32),
            pltpu.VMEM((group_slots, 2 * LANES), BF16),
            pltpu.VMEM((256, group_slots), BF16),
            pltpu.VMEM((rows // 2, 2 * LANES), F32),
            dma((n_copies,)), dma((n_copies,)),
            dma((n_mp,)), dma((n_mp,)),
            dma((4, n_dp)), dma((4, n_dp)),
            dma((n_mp,)), dma((n_mp,)),
            dma((n_dp,)), dma((n_dp,)),
        ],
        compiler_params=pltpu.CompilerParams(
            vmem_limit_bytes=58 << 20, collective_id=0, has_side_effects=True
        ),
        name="step",
    )(
        pooled_in, out_grad, pooled_grad, hot_ids, cold_owner.T, cold_rows, mlp_weight, mlp_accum,
        hot_table, hot_accum.reshape(hot // LANES, LANES),
        cold_table, cold_accum.reshape(rows // LANES, LANES),
    )
    new_weight, new_mlp_accum, new_hot, new_hot_accum, new_cold, new_cold_accum = outs
    return (
        new_weight,
        new_mlp_accum,
        new_hot,
        new_hot_accum.reshape(hot),
        new_cold,
        new_cold_accum.reshape(rows),
    )


def solution(mesh):
    split = P(("dp", "mp"), None)
    nx = ny = 4
    nz = mesh.shape["mp"] // 2
    return jax.shard_map(
        functools.partial(shards, nx, ny, nz),
        mesh=mesh,
        in_specs=(split,) * 8 + (P(), P(), split, P(("dp", "mp"))),
        out_specs=(split, split, P(), P(), split, P(("dp", "mp"))),
        check_vma=False,
    )
```

```python
import functools

import jax
import jax.numpy as jnp
from jax import lax
from jax.experimental import pallas as pl
from jax.experimental.pallas import tpu as pltpu
from jax.sharding import PartitionSpec as P

MESH = pl.DeviceIdType.MESH
RATE = 0.1
LANES = 128
F32 = jnp.float32
BF16 = jnp.bfloat16
I32 = jnp.int32
VMEM = pl.BlockSpec(memory_space=pltpu.VMEM)


SPLITS = 2
STEPS = 2

PLAN = (
    ("cores",), ("far", 0), ("far", 1), ("near", 0), ("near", 1), ("bucket", 0),
    ("far", 2), ("far", 3), ("near", 2), ("near", 3), ("bucket", 1), ("bucket", 2),
    ("own", 0), ("own", 1), ("own", 2), ("own", 3), ("join", 0), ("join", 1), ("bucket", 3), ("join", 2), ("join", 3),
    ("numbers_on",), ("hot_product",), ("forward", 0), ("numbers_in",), ("hot_scatter", "x"), ("forward", 1),
    ("hot_scatter", "y"), ("end", 0), ("end", 1), ("hot_scatter", "z"), ("end", 2), ("end", 3), ("gather", 0),
    ("join2", 0), ("join2", 1), ("join2", 2), ("join2", 3), ("forward", 2), ("hot_gather", "z"),
    ("end2", 0), ("end2", 1), ("along_z", 0), ("end2", 2), ("end2", 3), ("along_z", 1), ("gather", 1),
    ("hot_gather", "y"), ("forward", 3), ("end_z", 0), ("end_z", 1), ("hot_gather", "x"), ("gather", 2),
    ("weights", 0), ("weights", 1), ("hot_gather", "core"), ("gather", 3), ("hot_wait",),
)


def iota(shape, axis):
    return lax.broadcasted_iota(I32, shape, axis)


def onehot(rows, values):
    number = iota((rows, values.shape[1]), 0).astype(F32).astype(BF16)
    match = number == jnp.broadcast_to(values.astype(F32).astype(BF16), number.shape)
    return jnp.where(match, jnp.ones_like(number), jnp.zeros_like(number))


def lookup(values, table):
    out = jnp.zeros_like(values)
    for at, entry in enumerate(table):
        out = jnp.where(values == at, entry, out)
    return out


def dot(a, b):
    return lax.dot_general(a, b, (((1,), (0,)), ((), ())), preferred_element_type=F32)


def dot_t(a, b):
    return lax.dot_general(a, b, (((0,), (0,)), ((), ())), preferred_element_type=F32)


def adagrad_block(table, accum_row, grad):
    eye = iota((LANES, LANES), 0) == iota((LANES, LANES), 1)
    accum = jnp.sum(jnp.where(eye, accum_row, 0.0), axis=1, keepdims=True)
    new_accum = accum + jnp.sum(grad * grad, axis=1, keepdims=True) * (1.0 / LANES)
    new_table = table - grad * (RATE / jnp.sqrt(new_accum))
    new_row = jnp.sum(jnp.where(eye, new_accum, 0.0), axis=0, keepdims=True)
    return new_table, new_row


def dot_nt(a, b):
    return lax.dot_general(a, b, (((1,), (1,)), ((), ())), preferred_element_type=F32)


def split_columns(rhs, at, grad, upper):
    zero = jnp.zeros_like(grad)
    rows = grad.shape[0]
    rhs[at : at + rows, :LANES] = jnp.where(upper, zero, grad)
    rhs[at : at + rows, LANES:] = jnp.where(upper, grad, zero)


def step_kernel(
    nx, ny, nz, splits, cap, factor,
    x_ref, g_ref, pg_ref, hid_ref, own_ref, row_ref,
    wg_ref, hsum, cold,
    xp, gp, prod, recv1, recv2, sums, recv3, total, last,
    hot_rhs, hot_at, hpart, hp, hx, hy, hz,
    rank_row, own_row, rhs, lhs, send_buf, mid, fin, idsend, idmid, idout, idfin, ids, arhs, alhs,
    ss, rs, s1, r1, s2, r2, t1, q1, t2, q2,
):
    features, samples = hid_ref.shape
    n_dp, n_mp = nx * ny, nz * 2
    devices = n_dp * n_mp
    deep = cap // 2
    dp, mp = lax.axis_index("dp"), lax.axis_index("mp")
    x, y = lax.div(dp, ny), lax.rem(dp, ny)
    z, c = lax.div(mp, 2), lax.rem(mp, 2)

    def at_x(j):
        return (lax.rem(x + j, nx) * ny + y, mp)

    def at_y(j):
        return (x * ny + lax.rem(y + j, ny), mp)

    def at_z(j):
        return (dp, lax.rem(z + j, nz) * 2 + c)

    far_first = ((1, 2), (3, 2), (2, 1), (2, 3), (1, 1), (3, 3), (2, 0), (0, 2))
    far_first += ((1, 3), (3, 1), (2, 2), (0, 0), (1, 0), (3, 0), (0, 1), (0, 3))
    here_dp = far_first.index((0, 0))
    dp_slot = [far_first.index((i // ny, i % ny)) for i in range(n_dp)]

    def at_dp(i):
        dx, dy = far_first[i]
        return (lax.rem(x + dx, nx) * ny + lax.rem(y + dy, ny), mp)

    mid_z = nz // 2

    def at_mp(p):
        pz, pc = lax.div(p, 2), lax.rem(p, 2)
        jz = jnp.where(lax.rem(pz, 2) == 1, mid_z - lax.div(pz + 1, 2), mid_z + lax.div(pz, 2))
        return lax.rem(z + jz, nz) * 2 + lax.rem(c + pc, 2)

    here_slot = n_mp - 2
    partner = (dp, z * 2 + 1 - c)
    barrier = pltpu.get_barrier_semaphore()

    def greet_dp(i, _):
        pl.semaphore_signal(barrier, inc=1, device_id=(lax.rem(dp + i, n_dp), mp), device_id_type=MESH)
        return 0

    def greet_mp(j, _):
        pl.semaphore_signal(
            barrier, inc=1, device_id=(dp, lax.rem(mp + j, n_mp)), device_id_type=MESH
        )
        return 0

    lax.fori_loop(1, n_dp, greet_dp, 0)
    lax.fori_loop(1, n_mp, greet_mp, 0)

    line = LANES // features
    spread = jnp.concatenate(
        [
            jnp.broadcast_to(own_ref[:, r * LANES : (r + 1) * LANES], (line, LANES))
            for r in range(own_ref.shape[1] // LANES)
        ],
        axis=0,
    )
    keep = iota((samples, LANES), 1) // features == iota((samples, LANES), 0) % line
    pick = jnp.where(iota((features, LANES), 1) % features == iota((features, LANES), 0), 1.0, 0.0)
    owner = dot_nt(pick.astype(BF16), jnp.where(keep, spread, 0).astype(F32).astype(BF16)).astype(I32)
    to_mp = owner % n_mp
    jz = (to_mp // 2 - z + nz) % nz
    pz = jnp.where(jz > mid_z, 2 * (jz - mid_z), jnp.maximum(2 * (mid_z - jz) - 1, 0))
    to_mp = pz * 2 + (to_mp + c) % 2
    to_dp = owner // n_mp
    to_dp = lookup((to_dp // ny - x + nx) % nx * ny + (to_dp % ny - y + ny) % ny, dp_slot)
    quarters = 4
    each = n_dp // quarters
    own_row[...] = (to_dp // each * n_mp + to_mp) * each + to_dp % each
    id_place = to_mp * n_dp + to_dp
    earlier = jnp.where(
        iota((samples, samples), 0) < iota((samples, samples), 1), 1.0, 0.0
    ).astype(BF16)
    base = jnp.zeros((devices, 1), F32)
    for f in range(features):
        hot = onehot(devices, own_row[f : f + 1, :])
        hot32 = hot.astype(F32)
        before = dot(hot, earlier) + base
        rank_row[f : f + 1, :] = jnp.sum(hot32 * before, axis=0, keepdims=True)
        base = base + jnp.sum(hot32, axis=1, keepdims=True)

    rank_col = jnp.transpose(rank_row[...]).astype(I32)
    for f in range(features):
        odd = jnp.broadcast_to(rank_col[:, f : f + 1], (samples, LANES)) % 2 == 1
        split_columns(rhs, f * samples, pg_ref[:, f * LANES : (f + 1) * LANES], odd)
    slots = own_row[...] * deep + rank_row[...].astype(I32) // 2
    own_row[...] = slots

    pl.semaphore_wait(barrier, n_dp + n_mp - 2)

    copies = []

    def send(src, dst, device):
        k = len(copies)
        copy = pltpu.make_async_remote_copy(
            src_ref=src, dst_ref=dst, send_sem=ss.at[k], recv_sem=rs.at[k],
            device_id=device, device_id_type=MESH,
        )
        copy.start()
        copies.append(copy)
        return copy

    half = g_ref.shape[1] // 2
    quarter = half // 2
    rows = x_ref.shape[1]
    got_g = send(g_ref.at[:, pl.ds(pl.multiple_of((1 - c) * half, half), half)], gp, partner)
    got_x = send(x_ref, xp, partner)

    lane = iota((samples, LANES), 1)
    row_col = jnp.transpose(row_ref[...].astype(F32)).astype(I32)
    numbers = jnp.zeros((devices, LANES), F32)
    for f in range(features):
        rank = jnp.broadcast_to(rank_col[:, f : f + 1], (samples, LANES))
        row = jnp.broadcast_to(row_col[:, f : f + 1], (samples, LANES))
        spot = (rank % 2) * deep + rank // 2
        digit = jnp.where(lane < cap, row // 64 + 1, row % 64)
        digit = jnp.where((lane % cap == spot) & (lane < 2 * cap), digit, 0).astype(F32).astype(BF16)
        numbers += dot(onehot(devices, id_place[f : f + 1, :]), digit)
    idsend[...] = numbers

    def hop(src, dst, send_sem, recv_sem, device):
        return pltpu.make_async_remote_copy(
            src_ref=src, dst_ref=dst, send_sem=send_sem, recv_sem=recv_sem,
            device_id=device, device_id_type=MESH,
        )

    def ids_one(p):
        at = pl.ds(pl.multiple_of(p * n_dp, 8), n_dp)
        return hop(idsend.at[at], idmid.at[p], t1.at[p], q1.at[p], (dp, at_mp(p)))

    def cold_one(q, p):
        return hop(send_buf.at[q, p], mid.at[q, p], s1.at[q, p], r1.at[q, p], (dp, at_mp(p)))

    def ids_two(i):
        return hop(idout.at[i], idfin.at[i], t2.at[i], q2.at[i], at_dp(i))

    def cold_two(q, k):
        return hop(mid.at[q, :, k], fin.at[q, k], s2.at[q, k], r2.at[q, k], at_dp(q * each + k))

    def every_mp(act):
        def body(p, _):
            @pl.when(p != here_slot)
            def _():
                act(p)

            return 0

        lax.fori_loop(0, n_mp, body, 0)

    others = [i for i in range(n_dp) if i != here_dp]
    every_mp(lambda p: ids_one(p).start())
    blocks = samples // (each * deep)

    def bucket(m, _):
        for f in range(features):
            lhs[:, f * samples : (f + 1) * samples] = onehot(samples, own_row[f : f + 1, :] - m * samples)
        block = dot(lhs[...], rhs[...]).astype(BF16)
        q, first = lax.div(m * blocks, n_mp), lax.rem(m * blocks, n_mp)
        send_buf[q, pl.ds(first, blocks)] = block.reshape(blocks, each, deep, 2 * LANES)
        for k in range(blocks):
            p = first + k

            @pl.when(p != here_slot)
            def _():
                cold_one(q, p).start()

        return 0

    per_quarter = n_mp // blocks
    n = (nx, ny)
    chunk = rows // nx
    tile = rows // (nx * ny)
    here = (x, y)
    ends = ((at_x(1), at_x(nx - 1)), (at_y(1), at_y(ny - 1)))
    second = (ends[1], ends[0])
    width = quarter // splits
    todo = {}

    def bucket_quarter(q):
        lax.fori_loop(q * per_quarter, (q + 1) * per_quarter, bucket, 0)
        mid[q, here_slot] = send_buf[q, here_slot]

    def cores():
        got_g.wait_recv()
        got_x.wait_recv()

    def compute(u, rel):
        h, k = u % 2, u // 2
        dest = lax.rem(here[h] + rel, n[h])
        first = h * quarter + k * width
        cols = pl.ds(pl.multiple_of(c * half + first, width), width)
        for t in range(chunk // tile):
            if h == 0:
                at = dest * chunk + t * tile
            else:
                at = t * (rows // nx) + dest * tile
            at = pl.ds(pl.multiple_of(at, LANES), tile)
            prod[u, rel, t * tile : (t + 1) * tile, :] = dot_t(x_ref[:, at], g_ref[:, cols]) + dot_t(
                xp[:, at], gp[:, first : first + width]
            )

    def cut(rel, size, second_half):
        return (rel, size // 2 if second_half else 0, size // 2)

    def ring_far(key, part, buf, up, down, size):
        todo[key, "far"] = (
            send(part(*cut(2, size, False)), buf.at[0], up),
            send(part(*cut(2, size, True)), buf.at[1], down),
        )

    def ring_near(key, part, buf, up, down, size):
        todo[key, "near"] = (
            send(part(*cut(1, size, True)), buf.at[2], up),
            send(part(*cut(3, size, False)), buf.at[3], down),
        )

    def ring_join(key, part, buf, up, down, size):
        one, two = todo[key, "far"]
        one.wait_recv()
        ref = part(*cut(1, size, False))
        ref[...] = ref[...] + buf[0]
        one = send(ref, buf.at[4], up)
        two.wait_recv()
        ref = part(*cut(3, size, True))
        ref[...] = ref[...] + buf[1]
        todo[key, "join"] = (one, send(ref, buf.at[5], down))

    def ring_end(key, part, buf, up, down, size):
        for copy in todo[key, "near"] + todo[key, "join"]:
            copy.wait_recv()
        ref = part(*cut(0, size, False))
        ref[...] = ref[...] + buf[3] + buf[4]
        ref = part(*cut(0, size, True))
        ref[...] = ref[...] + buf[2] + buf[5]

    def part1(u):
        return lambda rel, start, size: prod.at[u, rel, pl.ds(start, size)]

    def part2(u):
        axis = 1 - u % 2

        def part(rel, start, size):
            dest = lax.rem(here[axis] + rel, n[axis])
            return prod.at[u, 0, pl.ds(pl.multiple_of(dest * tile + start, 8), size)]

        return part

    def one(u):
        return ((1, u), part1(u), recv1.at[u], *ends[u % 2], chunk)

    def two(u):
        return ((2, u), part2(u), recv2.at[u], *second[u % 2], tile)

    def far(u):
        compute(u, 2)
        ring_far(*one(u))

    def near(u):
        compute(u, 1)
        compute(u, 3)
        ring_near(*one(u))

    def own(u):
        compute(u, 0)

    def join(u):
        ring_join(*one(u))

    def end(u):
        ring_end(*one(u))
        ring_far(*two(u))
        ring_near(*two(u))

    def join2(u):
        ring_join(*two(u))

    band = tile // nz

    def end2(u):
        ring_end(*two(u))
        h, k = u % 2, u // 2
        at = pl.multiple_of(here[1 - h] * tile, 8)
        sums[k, :, h * width : (h + 1) * width] = prod[u, 0, pl.ds(at, tile), :]

    def along_z(k):
        todo["z", k] = [
            send(
                sums.at[k, pl.ds(pl.multiple_of(lax.rem(z + j, nz) * band, 8), band)],
                recv3.at[k, j - 1],
                at_z(j),
            )
            for j in range(1, nz)
        ]

    out_rows = band // 2

    def end_z(k):
        value = sums[k, pl.ds(pl.multiple_of(z * band, 8), band), :]
        for j in range(1, nz):
            todo["z", k][j - 1].wait_recv()
            value = value + recv3[k, j - 1]
        total[k] = value
        other_rows = pl.ds(pl.multiple_of((1 - c) * out_rows, 8), out_rows)
        todo["last", k] = send(total.at[k, other_rows], last.at[k], partner)

    def weights(k):
        todo["last", k].wait_recv()
        mine = total[k, pl.ds(pl.multiple_of(c * out_rows, 8), out_rows), :]
        other = last[k]
        for side in range(2):
            grad = jnp.where(c == side, mine, other) * factor
            for h in range(2):
                at = side * half + h * quarter + k * width
                wg_ref[:, at : at + width] = grad[:, h * width : (h + 1) * width]

    def at_first(j):
        return (jnp.where(c == 0, at_x(j)[0], at_y(j)[0]), mp)

    def at_second(j):
        return (jnp.where(c == 0, at_y(j)[0], at_x(j)[0]), mp)

    first, next_one = jnp.where(c == 0, x, y), jnp.where(c == 0, y, x)
    hot_rows = hp.shape[0]
    hrx, hry, hrz = hot_rows // nx, hot_rows // (nx * ny), hot_rows // (nx * ny * nz)
    base_x = pl.multiple_of(first * hrx, 8)
    base_y = pl.multiple_of(base_x + next_one * hry, 8)
    base_z = pl.multiple_of(base_y + z * hrz, 8)
    base_c = pl.multiple_of(c * hot_rows, 8)

    def hot_product():
        hot_row = hid_ref[...]
        hot_ids = jnp.transpose(hot_row.astype(F32)).astype(I32)
        hot_at[...] = jnp.where(hot_row >= hot_rows, hot_row - hot_rows, hot_row)
        for f in range(features):
            upper = jnp.broadcast_to(hot_ids[:, f : f + 1], (samples, LANES)) >= hot_rows
            split_columns(hot_rhs, f * samples, pg_ref[:, f * LANES : (f + 1) * LANES], upper)

        def hot_block(m, _):
            for f in range(features):
                lhs[:, f * samples : (f + 1) * samples] = onehot(samples, hot_at[f : f + 1, :] - m * samples)
            hpart[pl.ds(pl.multiple_of(m * samples, 8), samples), :] = dot(lhs[...], hot_rhs[...])
            return 0

        lax.fori_loop(0, hot_rows // samples, hot_block, 0)
        theirs = hpart.at[:, pl.ds(pl.multiple_of((1 - c) * LANES, LANES), LANES)]
        todo["hot"] = [send(theirs, hp, partner)]

    def hot_wait():
        for copy in todo["hot"]:
            copy.wait_recv()

    def hot_scatter(axis):
        hot_wait()
        if axis == "x":
            hp[...] = hp[...] + hpart[:, pl.ds(pl.multiple_of(c * LANES, LANES), LANES)]
            base, size, buf, me, count, at = 0, hrx, hx, first, nx, at_first
        elif axis == "y":
            ref = hp.at[pl.ds(base_x, hrx)]
            ref[...] = ref[...] + hx[0] + hx[1] + hx[2]
            base, size, buf, me, count, at = base_x, hry, hy, next_one, ny, at_second
        else:
            ref = hp.at[pl.ds(base_y, hry)]
            ref[...] = ref[...] + hy[0] + hy[1] + hy[2]
            base, size, buf, me, count, at = base_y, hrz, hz, z, nz, at_z
        todo["hot"] = [
            send(hp.at[pl.ds(pl.multiple_of(base + lax.rem(me + j, count) * size, 8), size)], buf.at[j - 1], at(j))
            for j in range(1, count)
        ]

    def hot_gather(axis):
        hot_wait()
        if axis == "z":
            got = hp[pl.ds(base_z, hrz), :]
            for j in range(1, nz):
                got = got + hz[j - 1]
            own_z = pl.multiple_of(base_c + base_z, 8)
            hsum[pl.ds(own_z, hrz), :] = got
            ref, peers = hsum.at[pl.ds(own_z, hrz)], [at_z(j) for j in range(1, nz)]
        elif axis == "y":
            ref = hsum.at[pl.ds(pl.multiple_of(base_c + base_y, 8), hry)]
            peers = [at_second(j) for j in range(1, ny)]
        elif axis == "x":
            ref = hsum.at[pl.ds(pl.multiple_of(base_c + base_x, 8), hrx)]
            peers = [at_first(j) for j in range(1, nx)]
        else:
            ref, peers = hsum.at[pl.ds(base_c, hot_rows)], [partner]
        todo["hot"] = [send(ref, ref, peer) for peer in peers]

    def numbers_on():
        every_mp(lambda p: ids_one(p).wait_recv())
        idmid[here_slot] = idsend[here_slot * n_dp : (here_slot + 1) * n_dp, :]
        for i in range(n_dp):
            idout[i] = jnp.concatenate([idmid[p, i : i + 1, :] for p in range(n_mp)], axis=0)
        for i in others:
            ids_two(i).start()

    band8 = LANES // deep

    def numbers_in():
        for i in others:
            ids_two(i).wait_recv()
        idfin[here_dp] = idout[here_dp]
        digits = idfin[...].reshape(devices, LANES).astype(BF16)
        at_lane, at_digit = iota((LANES, 2 * LANES), 1), iota((LANES, 2 * LANES), 0)
        want = (at_lane // LANES) * deep + at_lane % deep
        high = dot(digits, jnp.where(at_digit == want, 1.0, 0.0).astype(BF16))
        low = dot(digits, jnp.where(at_digit == want + cap, 1.0, 0.0).astype(BF16))
        numbers = high * 64.0 + low - 64.0
        keep = (iota(numbers.shape, 1) % LANES) // deep == iota(numbers.shape, 0) % band8
        numbers = jnp.where(keep, numbers, 0.0)
        numbers = jnp.sum(numbers.reshape(devices // band8, band8, 2 * LANES), axis=1)
        ids[...] = numbers.astype(I32)

    def forward(q):
        every_mp(lambda p: cold_one(q, p).wait_recv())
        for k in range(each):
            if q * each + k == here_dp:
                fin[q, k] = mid[q, :, k]
            else:
                cold_two(q, k).start()

    cold_half = cold.shape[0]
    per = each * n_mp * deep
    pieces = per // LANES
    step = 256

    def gather(g):
        for k in range(each):
            if g * each + k != here_dp:
                cold_two(g, k).wait_recv()
        eye = iota((LANES, LANES), 0) == iota((LANES, LANES), 1)
        ones = jnp.ones((LANES, LANES), BF16)
        for q in range(pieces):
            run = q % (n_mp // band8) * band8
            grads = fin[g, q // (n_mp // band8), run : run + band8].reshape(LANES, 2 * LANES)
            for k in range(2):
                number = ids[g * pieces + q : g * pieces + q + 1, k * LANES : (k + 1) * LANES]
                upper = jnp.where(number >= cold_half, 1.0, 0.0)
                column = dot(jnp.where(eye, upper, 0.0).astype(BF16), ones)
                split_columns(arhs, k * per + q * LANES, grads[:, k * LANES : (k + 1) * LANES], column > 0.5)

        def block(m, _):
            for q in range(pieces):
                for k in range(2):
                    number = ids[g * pieces + q : g * pieces + q + 1, k * LANES : (k + 1) * LANES]
                    number = jnp.where(number >= cold_half, number - cold_half, number)
                    at = k * per + q * LANES
                    alhs[:, at : at + LANES] = onehot(step, number - m * step)
            at = pl.ds(pl.multiple_of(m * step, 8), step)
            part = dot(alhs[...], arhs[...])
            if g == 0:
                cold[at, :] = part
            else:
                cold[at, :] = cold[at, :] + part
            return 0

        lax.fori_loop(0, cold_half // step, block, 0)

    for action, *given in PLAN:
        {
            "bucket": bucket_quarter, "cores": cores, "far": far, "near": near, "own": own, "join": join,
            "end": end, "join2": join2, "end2": end2, "along_z": along_z, "end_z": end_z, "weights": weights,
            "hot_product": hot_product, "hot_scatter": hot_scatter, "hot_gather": hot_gather, "hot_wait": hot_wait,
            "numbers_on": numbers_on, "numbers_in": numbers_in, "forward": forward, "gather": gather,
        }[action](*given)

    for copy in copies:
        copy.wait_send()
    every_mp(lambda p: ids_one(p).wait_send())
    for q in range(quarters):
        every_mp(lambda p: cold_one(q, p).wait_send())
    for i in others:
        ids_two(i).wait_send()
        cold_two(i // each, i % each).wait_send()


def update_kernel(
    wg_ref, hot_ref, cold_ref, w_ref, a_ref, ht_ref, ha_ref, ct_ref, ca_ref,
    nw_ref, na_ref, nh_ref, nha_ref, nc_ref, nca_ref,
):
    m, steps = pl.program_id(0), pl.num_programs(0)

    @pl.when(m == 0)
    def _():
        grad = wg_ref[...]
        accum = a_ref[...] + grad * grad
        na_ref[...] = accum
        nw_ref[...] = w_ref[...] - RATE * grad / jnp.sqrt(accum)

    parts = hot_ref.shape[0] // LANES
    for part in range(parts):
        at, line = slice(part * LANES, (part + 1) * LANES), pl.ds(m * parts + part, 1)
        nh_ref[at, :], nha_ref[line, :] = adagrad_block(ht_ref[at, :], ha_ref[line, :], hot_ref[at, :])
    parts = cold_ref.shape[0] // LANES
    for upper in range(2):
        for part in range(parts):
            at, line = slice(part * LANES, (part + 1) * LANES), pl.ds((upper * steps + m) * parts + part, 1)
            grad = cold_ref[at, upper * LANES : (upper + 1) * LANES]
            nc_ref[upper, at, :], nca_ref[line, :] = adagrad_block(ct_ref[upper, at, :], ca_ref[line, :], grad)


def shards(
    nx, ny, nz,
    pooled_in, out_grad, pooled_grad, hot_ids, cold_owner, cold_rows,
    mlp_weight, mlp_accum, hot_table, hot_accum, cold_table, cold_accum,
):
    n_dp, n_mp = nx * ny, nz * 2
    devices = n_dp * n_mp
    samples, features = hot_ids.shape
    hid = pooled_in.shape[1]
    hot = hot_table.shape[0]
    rows = cold_table.shape[0]
    lookups = samples * features
    cap = 2 * lookups // devices
    deep = cap // 2
    group_slots = 2 * (n_dp * (n_mp // 4) * deep)
    quarter = hid // 4
    chunk, tile = hid // nx, hid // (nx * ny)
    band = tile // nz
    half_hot = hot // 2
    hrx, hry, hrz = half_hot // nx, half_hot // (nx * ny), half_hot // (nx * ny * nz)
    pieces = 2 * SPLITS
    width = quarter // SPLITS
    n_copies = 4 + pieces * 6 * 2 + SPLITS * nz + 2 * (nx - 1 + ny - 1 + nz - 1)
    dma = pltpu.SemaphoreType.DMA
    weight_grad, hot_grad, cold_grad = pl.pallas_call(
        functools.partial(step_kernel, nx, ny, nz, SPLITS, cap, float(samples * devices) ** (-0.5)),
        out_shape=(
            jax.ShapeDtypeStruct(mlp_weight.shape, F32),
            jax.ShapeDtypeStruct(hot_table.shape, F32),
            jax.ShapeDtypeStruct((rows // 2, 2 * LANES), F32),
        ),
        in_specs=[VMEM] * 6,
        out_specs=(VMEM,) * 3,
        scratch_shapes=[
            pltpu.VMEM((samples, hid), BF16),
            pltpu.VMEM((samples, hid // 2), BF16),
            pltpu.VMEM((pieces, 4, chunk, width), F32),
            pltpu.VMEM((pieces, 6, chunk // 2, width), F32),
            pltpu.VMEM((pieces, 6, tile // 2, width), F32),
            pltpu.VMEM((SPLITS, tile, 2 * width), F32),
            pltpu.VMEM((SPLITS, nz - 1, band, 2 * width), F32),
            pltpu.VMEM((SPLITS, band, 2 * width), F32),
            pltpu.VMEM((SPLITS, band // 2, 2 * width), F32),
            pltpu.VMEM((lookups, 2 * LANES), BF16),
            pltpu.VMEM((features, samples), I32),
            pltpu.VMEM((half_hot, 2 * LANES), F32),
            pltpu.VMEM((half_hot, LANES), F32),
            pltpu.VMEM((nx - 1, hrx, LANES), F32),
            pltpu.VMEM((ny - 1, hry, LANES), F32),
            pltpu.VMEM((nz - 1, hrz, LANES), F32),
            pltpu.VMEM((features, samples), F32),
            pltpu.VMEM((features, samples), I32),
            pltpu.VMEM((lookups, 2 * LANES), BF16),
            pltpu.VMEM((samples, lookups), BF16),
            pltpu.VMEM((4, n_mp, n_dp // 4, deep, 2 * LANES), BF16),
            pltpu.VMEM((4, n_mp, n_dp // 4, deep, 2 * LANES), BF16),
            pltpu.VMEM((4, n_dp // 4, n_mp, deep, 2 * LANES), BF16),
            pltpu.VMEM((devices, LANES), F32),
            pltpu.VMEM((n_mp, n_dp, LANES), F32),
            pltpu.VMEM((n_dp, n_mp, LANES), F32),
            pltpu.VMEM((n_dp, n_mp, LANES), F32),
            pltpu.VMEM((devices * deep // LANES, 2 * LANES), I32),
            pltpu.VMEM((group_slots, 2 * LANES), BF16),
            pltpu.VMEM((256, group_slots), BF16),
            dma((n_copies,)), dma((n_copies,)),
            dma((4, n_mp)), dma((4, n_mp)),
            dma((4, n_dp // 4)), dma((4, n_dp // 4)),
            dma((n_mp,)), dma((n_mp,)),
            dma((n_dp,)), dma((n_dp,)),
        ],
        compiler_params=pltpu.CompilerParams(
            vmem_limit_bytes=58 << 20, collective_id=0, has_side_effects=True
        ),
        name="step",
    )(
        pooled_in, out_grad, pooled_grad, hot_ids.T, cold_owner.T, cold_rows.T
    )

    steps = STEPS
    whole = lambda *shape: pl.BlockSpec(shape, lambda m: (0,) * len(shape))
    hot_block = pl.BlockSpec((hot // steps, LANES), lambda m: (m, 0))
    cold_block = pl.BlockSpec((2, rows // 2 // steps, LANES), lambda m: (0, m, 0))
    weight = whole(*mlp_weight.shape)
    hot_line, cold_line = whole(hot // LANES, LANES), whole(rows // LANES, LANES)
    new_weight, new_mlp_accum, new_hot, new_hot_accum, new_cold, new_cold_accum = pl.pallas_call(
        update_kernel,
        grid=(steps,),
        out_shape=(
            jax.ShapeDtypeStruct(mlp_weight.shape, F32),
            jax.ShapeDtypeStruct(mlp_accum.shape, F32),
            jax.ShapeDtypeStruct(hot_table.shape, F32),
            jax.ShapeDtypeStruct((hot // LANES, LANES), F32),
            jax.ShapeDtypeStruct((2, rows // 2, LANES), F32),
            jax.ShapeDtypeStruct((rows // LANES, LANES), F32),
        ),
        in_specs=[
            weight, hot_block, pl.BlockSpec((rows // 2 // steps, 2 * LANES), lambda m: (m, 0)),
            weight, weight, hot_block, hot_line, cold_block, cold_line,
        ],
        out_specs=(weight, weight, hot_block, hot_line, cold_block, cold_line),
        name="update",
    )(
        weight_grad, hot_grad, cold_grad, mlp_weight, mlp_accum,
        hot_table, hot_accum.reshape(hot // LANES, LANES),
        cold_table.reshape(2, rows // 2, LANES), cold_accum.reshape(rows // LANES, LANES),
    )
    return (
        new_weight,
        new_mlp_accum,
        new_hot,
        new_hot_accum.reshape(hot),
        new_cold.reshape(rows, LANES),
        new_cold_accum.reshape(rows),
    )


def solution(mesh):
    split = P(("dp", "mp"), None)
    nx = ny = 4
    nz = mesh.shape["mp"] // 2
    return jax.shard_map(
        functools.partial(shards, nx, ny, nz),
        mesh=mesh,
        in_specs=(split,) * 8 + (P(), P(), split, P(("dp", "mp"))),
        out_specs=(split, split, P(), P(), split, P(("dp", "mp"))),
        check_vma=False,
    )
```

```python
import functools

import jax
import jax.numpy as jnp
from jax import lax
from jax.experimental import pallas as pl
from jax.experimental.pallas import tpu as pltpu
from jax.sharding import PartitionSpec as P

MESH = pl.DeviceIdType.MESH
RATE = 0.1
LANES = 128
F32 = jnp.float32
BF16 = jnp.bfloat16
I32 = jnp.int32
VMEM = pl.BlockSpec(memory_space=pltpu.VMEM)


SPLITS = 2
STEPS = 2

PLAN = (
    ("bucket", 0), ("cores",), ("far", 0), ("far", 1), ("near", 0), ("near", 1),
    ("far", 2), ("far", 3), ("near", 2), ("near", 3), ("bucket", 1), ("bucket", 2),
    ("own", 0), ("own", 1), ("own", 2), ("own", 3), ("join", 0), ("join", 1), ("bucket", 3), ("join", 2), ("join", 3),
    ("numbers_on",), ("hot_product",), ("forward", 0), ("numbers_in",), ("hot_scatter", "x"), ("forward", 1),
    ("hot_scatter", "y"), ("end", 0), ("end", 1), ("hot_scatter", "z"), ("end", 2), ("end", 3), ("gather", 0),
    ("join2", 0), ("join2", 1), ("join2", 2), ("join2", 3), ("forward", 2), ("hot_gather", "z"),
    ("end2", 0), ("end2", 1), ("along_z", 0), ("end2", 2), ("end2", 3), ("along_z", 1), ("gather", 1),
    ("hot_gather", "y"), ("forward", 3), ("end_z", 0), ("end_z", 1), ("hot_gather", "x"), ("gather", 2),
    ("weights", 0), ("weights", 1), ("hot_gather", "core"), ("gather", 3), ("hot_wait",),
)


def iota(shape, axis):
    return lax.broadcasted_iota(I32, shape, axis)


def onehot(rows, values):
    number = iota((rows, values.shape[1]), 0).astype(F32).astype(BF16)
    match = number == jnp.broadcast_to(values.astype(F32).astype(BF16), number.shape)
    return jnp.where(match, jnp.ones_like(number), jnp.zeros_like(number))


def lookup(values, table):
    out = jnp.zeros_like(values)
    for at, entry in enumerate(table):
        out = jnp.where(values == at, entry, out)
    return out


def dot(a, b):
    return lax.dot_general(a, b, (((1,), (0,)), ((), ())), preferred_element_type=F32)


def dot_t(a, b):
    return lax.dot_general(a, b, (((0,), (0,)), ((), ())), preferred_element_type=F32)


def adagrad_block(table, accum_row, grad):
    eye = iota((LANES, LANES), 0) == iota((LANES, LANES), 1)
    accum = jnp.sum(jnp.where(eye, accum_row, 0.0), axis=1, keepdims=True)
    new_accum = accum + jnp.sum(grad * grad, axis=1, keepdims=True) * (1.0 / LANES)
    new_table = table - grad * (RATE / jnp.sqrt(new_accum))
    new_row = jnp.sum(jnp.where(eye, new_accum, 0.0), axis=0, keepdims=True)
    return new_table, new_row


def dot_nt(a, b):
    return lax.dot_general(a, b, (((1,), (1,)), ((), ())), preferred_element_type=F32)


def split_columns(rhs, at, grad, upper):
    zero = jnp.zeros_like(grad)
    rows = grad.shape[0]
    rhs[at : at + rows, :LANES] = jnp.where(upper, zero, grad)
    rhs[at : at + rows, LANES:] = jnp.where(upper, grad, zero)


def step_kernel(
    nx, ny, nz, splits, cap, factor,
    x_ref, g_ref, pg_ref, hid_ref, own_ref, row_ref,
    wg_ref, hsum, cold,
    xp, gp, prod, recv1, recv2, sums, recv3, total, last,
    hot_rhs, hot_at, hpart, hp, hx, hy, hz,
    rank_row, own_row, rhs, lhs, send_buf, mid, fin, idsend, idmid, idout, idfin, ids, arhs, alhs,
    ss, rs, s1, r1, s2, r2, t1, q1, t2, q2,
):
    features, samples = hid_ref.shape
    n_dp, n_mp = nx * ny, nz * 2
    devices = n_dp * n_mp
    deep = cap // 2
    dp, mp = lax.axis_index("dp"), lax.axis_index("mp")
    x, y = lax.div(dp, ny), lax.rem(dp, ny)
    z, c = lax.div(mp, 2), lax.rem(mp, 2)

    def at_x(j):
        return (lax.rem(x + j, nx) * ny + y, mp)

    def at_y(j):
        return (x * ny + lax.rem(y + j, ny), mp)

    def at_z(j):
        return (dp, lax.rem(z + j, nz) * 2 + c)

    far_first = ((1, 2), (3, 2), (2, 1), (2, 3), (1, 1), (3, 3), (2, 0), (0, 2))
    far_first += ((1, 3), (3, 1), (2, 2), (0, 0), (1, 0), (3, 0), (0, 1), (0, 3))
    here_dp = far_first.index((0, 0))
    dp_slot = [far_first.index((i // ny, i % ny)) for i in range(n_dp)]

    def at_dp(i):
        dx, dy = far_first[i]
        return (lax.rem(x + dx, nx) * ny + lax.rem(y + dy, ny), mp)

    mid_z = nz // 2

    def at_mp(p):
        pz, pc = lax.div(p, 2), lax.rem(p, 2)
        jz = jnp.where(lax.rem(pz, 2) == 1, mid_z - lax.div(pz + 1, 2), mid_z + lax.div(pz, 2))
        return lax.rem(z + jz, nz) * 2 + lax.rem(c + pc, 2)

    here_slot = n_mp - 2
    partner = (dp, z * 2 + 1 - c)
    barrier = pltpu.get_barrier_semaphore()

    def greet_dp(i, _):
        pl.semaphore_signal(barrier, inc=1, device_id=(lax.rem(dp + i, n_dp), mp), device_id_type=MESH)
        return 0

    def greet_mp(j, _):
        pl.semaphore_signal(
            barrier, inc=1, device_id=(dp, lax.rem(mp + j, n_mp)), device_id_type=MESH
        )
        return 0

    lax.fori_loop(1, n_dp, greet_dp, 0)
    lax.fori_loop(1, n_mp, greet_mp, 0)

    line = LANES // features
    spread = jnp.concatenate(
        [
            jnp.broadcast_to(own_ref[:, r * LANES : (r + 1) * LANES], (line, LANES))
            for r in range(own_ref.shape[1] // LANES)
        ],
        axis=0,
    )
    keep = iota((samples, LANES), 1) // features == iota((samples, LANES), 0) % line
    pick = jnp.where(iota((features, LANES), 1) % features == iota((features, LANES), 0), 1.0, 0.0)
    owner = dot_nt(pick.astype(BF16), jnp.where(keep, spread, 0).astype(F32).astype(BF16)).astype(I32)
    to_mp = owner % n_mp
    jz = (to_mp // 2 - z + nz) % nz
    pz = jnp.where(jz > mid_z, 2 * (jz - mid_z), jnp.maximum(2 * (mid_z - jz) - 1, 0))
    to_mp = pz * 2 + (to_mp + c) % 2
    to_dp = owner // n_mp
    to_dp = lookup((to_dp // ny - x + nx) % nx * ny + (to_dp % ny - y + ny) % ny, dp_slot)
    quarters = 4
    each = n_dp // quarters
    own_row[...] = (to_dp // each * n_mp + to_mp) * each + to_dp % each
    id_place = to_mp * n_dp + to_dp
    earlier = jnp.where(
        iota((samples, samples), 0) < iota((samples, samples), 1), 1.0, 0.0
    ).astype(BF16)
    base = jnp.zeros((devices, 1), F32)
    for f in range(features):
        hot = onehot(devices, own_row[f : f + 1, :])
        hot32 = hot.astype(F32)
        before = dot(hot, earlier) + base
        rank_row[f : f + 1, :] = jnp.sum(hot32 * before, axis=0, keepdims=True)
        base = base + jnp.sum(hot32, axis=1, keepdims=True)

    rank_col = jnp.transpose(rank_row[...]).astype(I32)
    for f in range(features):
        odd = jnp.broadcast_to(rank_col[:, f : f + 1], (samples, LANES)) % 2 == 1
        split_columns(rhs, f * samples, pg_ref[:, f * LANES : (f + 1) * LANES], odd)
    slots = own_row[...] * deep + rank_row[...].astype(I32) // 2
    own_row[...] = slots

    pl.semaphore_wait(barrier, n_dp + n_mp - 2)

    copies = []

    def send(src, dst, device):
        k = len(copies)
        copy = pltpu.make_async_remote_copy(
            src_ref=src, dst_ref=dst, send_sem=ss.at[k], recv_sem=rs.at[k],
            device_id=device, device_id_type=MESH,
        )
        copy.start()
        copies.append(copy)
        return copy

    half = g_ref.shape[1] // 2
    quarter = half // 2
    rows = x_ref.shape[1]
    got_g = send(g_ref.at[:, pl.ds(pl.multiple_of((1 - c) * half, half), half)], gp, partner)
    got_x = send(x_ref, xp, partner)

    lane = iota((samples, LANES), 1)
    row_col = jnp.transpose(row_ref[...].astype(F32)).astype(I32)
    numbers = jnp.zeros((devices, LANES), F32)
    for f in range(features):
        rank = jnp.broadcast_to(rank_col[:, f : f + 1], (samples, LANES))
        row = jnp.broadcast_to(row_col[:, f : f + 1], (samples, LANES))
        spot = (rank % 2) * deep + rank // 2
        digit = jnp.where(lane < cap, row // 64 + 1, row % 64)
        digit = jnp.where((lane % cap == spot) & (lane < 2 * cap), digit, 0).astype(F32).astype(BF16)
        numbers += dot(onehot(devices, id_place[f : f + 1, :]), digit)
    idsend[...] = numbers

    def hop(src, dst, send_sem, recv_sem, device):
        return pltpu.make_async_remote_copy(
            src_ref=src, dst_ref=dst, send_sem=send_sem, recv_sem=recv_sem,
            device_id=device, device_id_type=MESH,
        )

    def ids_one(p):
        at = pl.ds(pl.multiple_of(p * n_dp, 8), n_dp)
        return hop(idsend.at[at], idmid.at[p], t1.at[p], q1.at[p], (dp, at_mp(p)))

    def cold_one(q, p):
        return hop(send_buf.at[q, p], mid.at[q, p], s1.at[q, p], r1.at[q, p], (dp, at_mp(p)))

    def ids_two(i):
        return hop(idout.at[i], idfin.at[i], t2.at[i], q2.at[i], at_dp(i))

    def cold_two(q, k):
        return hop(mid.at[q, :, k], fin.at[q, k], s2.at[q, k], r2.at[q, k], at_dp(q * each + k))

    def every_mp(act):
        def body(p, _):
            @pl.when(p != here_slot)
            def _():
                act(p)

            return 0

        lax.fori_loop(0, n_mp, body, 0)

    others = [i for i in range(n_dp) if i != here_dp]
    every_mp(lambda p: ids_one(p).start())
    blocks = samples // (each * deep)

    def bucket(m, _):
        for f in range(features):
            lhs[:, f * samples : (f + 1) * samples] = onehot(samples, own_row[f : f + 1, :] - m * samples)
        block = dot(lhs[...], rhs[...]).astype(BF16)
        q, first = lax.div(m * blocks, n_mp), lax.rem(m * blocks, n_mp)
        send_buf[q, pl.ds(first, blocks)] = block.reshape(blocks, each, deep, 2 * LANES)
        for k in range(blocks):
            p = first + k

            @pl.when(p != here_slot)
            def _():
                cold_one(q, p).start()

        return 0

    per_quarter = n_mp // blocks
    n = (nx, ny)
    chunk = rows // nx
    tile = rows // (nx * ny)
    here = (x, y)
    ends = ((at_x(1), at_x(nx - 1)), (at_y(1), at_y(ny - 1)))
    second = (ends[1], ends[0])
    width = quarter // splits
    todo = {}

    def bucket_quarter(q):
        lax.fori_loop(q * per_quarter, (q + 1) * per_quarter, bucket, 0)
        mid[q, here_slot] = send_buf[q, here_slot]

    def cores():
        got_g.wait_recv()
        got_x.wait_recv()

    def compute(u, rel):
        h, k = u % 2, u // 2
        dest = lax.rem(here[h] + rel, n[h])
        first = h * quarter + k * width
        cols = pl.ds(pl.multiple_of(c * half + first, width), width)
        for t in range(chunk // tile):
            if h == 0:
                at = dest * chunk + t * tile
            else:
                at = t * (rows // nx) + dest * tile
            at = pl.ds(pl.multiple_of(at, LANES), tile)
            prod[u, rel, t * tile : (t + 1) * tile, :] = dot_t(x_ref[:, at], g_ref[:, cols]) + dot_t(
                xp[:, at], gp[:, first : first + width]
            )

    def cut(rel, size, second_half):
        return (rel, size // 2 if second_half else 0, size // 2)

    def ring_far(key, part, buf, up, down, size):
        todo[key, "far"] = (
            send(part(*cut(2, size, False)), buf.at[0], up),
            send(part(*cut(2, size, True)), buf.at[1], down),
        )

    def ring_near(key, part, buf, up, down, size):
        todo[key, "near"] = (
            send(part(*cut(1, size, True)), buf.at[2], up),
            send(part(*cut(3, size, False)), buf.at[3], down),
        )

    def ring_join(key, part, buf, up, down, size):
        one, two = todo[key, "far"]
        one.wait_recv()
        ref = part(*cut(1, size, False))
        ref[...] = ref[...] + buf[0]
        one = send(ref, buf.at[4], up)
        two.wait_recv()
        ref = part(*cut(3, size, True))
        ref[...] = ref[...] + buf[1]
        todo[key, "join"] = (one, send(ref, buf.at[5], down))

    def ring_end(key, part, buf, up, down, size):
        for copy in todo[key, "near"] + todo[key, "join"]:
            copy.wait_recv()
        ref = part(*cut(0, size, False))
        ref[...] = ref[...] + buf[3] + buf[4]
        ref = part(*cut(0, size, True))
        ref[...] = ref[...] + buf[2] + buf[5]

    def part1(u):
        return lambda rel, start, size: prod.at[u, rel, pl.ds(start, size)]

    def part2(u):
        axis = 1 - u % 2

        def part(rel, start, size):
            dest = lax.rem(here[axis] + rel, n[axis])
            return prod.at[u, 0, pl.ds(pl.multiple_of(dest * tile + start, 8), size)]

        return part

    def one(u):
        return ((1, u), part1(u), recv1.at[u], *ends[u % 2], chunk)

    def two(u):
        return ((2, u), part2(u), recv2.at[u], *second[u % 2], tile)

    def far(u):
        compute(u, 2)
        ring_far(*one(u))

    def near(u):
        compute(u, 1)
        compute(u, 3)
        ring_near(*one(u))

    def own(u):
        compute(u, 0)

    def join(u):
        ring_join(*one(u))

    def end(u):
        ring_end(*one(u))
        ring_far(*two(u))
        ring_near(*two(u))

    def join2(u):
        ring_join(*two(u))

    band = tile // nz

    def end2(u):
        ring_end(*two(u))
        h, k = u % 2, u // 2
        at = pl.multiple_of(here[1 - h] * tile, 8)
        sums[k, :, h * width : (h + 1) * width] = prod[u, 0, pl.ds(at, tile), :]

    def along_z(k):
        todo["z", k] = [
            send(
                sums.at[k, pl.ds(pl.multiple_of(lax.rem(z + j, nz) * band, 8), band)],
                recv3.at[k, j - 1],
                at_z(j),
            )
            for j in range(1, nz)
        ]

    out_rows = band // 2

    def end_z(k):
        value = sums[k, pl.ds(pl.multiple_of(z * band, 8), band), :]
        for j in range(1, nz):
            todo["z", k][j - 1].wait_recv()
            value = value + recv3[k, j - 1]
        total[k] = value
        other_rows = pl.ds(pl.multiple_of((1 - c) * out_rows, 8), out_rows)
        todo["last", k] = send(total.at[k, other_rows], last.at[k], partner)

    def weights(k):
        todo["last", k].wait_recv()
        mine = total[k, pl.ds(pl.multiple_of(c * out_rows, 8), out_rows), :]
        other = last[k]
        for side in range(2):
            grad = jnp.where(c == side, mine, other) * factor
            for h in range(2):
                at = side * half + h * quarter + k * width
                wg_ref[:, at : at + width] = grad[:, h * width : (h + 1) * width]

    def at_first(j):
        return (jnp.where(c == 0, at_x(j)[0], at_y(j)[0]), mp)

    def at_second(j):
        return (jnp.where(c == 0, at_y(j)[0], at_x(j)[0]), mp)

    first, next_one = jnp.where(c == 0, x, y), jnp.where(c == 0, y, x)
    hot_rows = hp.shape[0]
    hrx, hry, hrz = hot_rows // nx, hot_rows // (nx * ny), hot_rows // (nx * ny * nz)
    base_x = pl.multiple_of(first * hrx, 8)
    base_y = pl.multiple_of(base_x + next_one * hry, 8)
    base_z = pl.multiple_of(base_y + z * hrz, 8)
    base_c = pl.multiple_of(c * hot_rows, 8)

    def hot_product():
        hot_row = hid_ref[...]
        hot_ids = jnp.transpose(hot_row.astype(F32)).astype(I32)
        hot_at[...] = jnp.where(hot_row >= hot_rows, hot_row - hot_rows, hot_row)
        for f in range(features):
            upper = jnp.broadcast_to(hot_ids[:, f : f + 1], (samples, LANES)) >= hot_rows
            split_columns(hot_rhs, f * samples, pg_ref[:, f * LANES : (f + 1) * LANES], upper)

        def hot_block(m, _):
            for f in range(features):
                lhs[:, f * samples : (f + 1) * samples] = onehot(samples, hot_at[f : f + 1, :] - m * samples)
            hpart[pl.ds(pl.multiple_of(m * samples, 8), samples), :] = dot(lhs[...], hot_rhs[...])
            return 0

        lax.fori_loop(0, hot_rows // samples, hot_block, 0)
        theirs = hpart.at[:, pl.ds(pl.multiple_of((1 - c) * LANES, LANES), LANES)]
        todo["hot"] = [send(theirs, hp, partner)]

    def hot_wait():
        for copy in todo["hot"]:
            copy.wait_recv()

    def hot_scatter(axis):
        hot_wait()
        if axis == "x":
            hp[...] = hp[...] + hpart[:, pl.ds(pl.multiple_of(c * LANES, LANES), LANES)]
            base, size, buf, me, count, at = 0, hrx, hx, first, nx, at_first
        elif axis == "y":
            ref = hp.at[pl.ds(base_x, hrx)]
            ref[...] = ref[...] + hx[0] + hx[1] + hx[2]
            base, size, buf, me, count, at = base_x, hry, hy, next_one, ny, at_second
        else:
            ref = hp.at[pl.ds(base_y, hry)]
            ref[...] = ref[...] + hy[0] + hy[1] + hy[2]
            base, size, buf, me, count, at = base_y, hrz, hz, z, nz, at_z
        todo["hot"] = [
            send(hp.at[pl.ds(pl.multiple_of(base + lax.rem(me + j, count) * size, 8), size)], buf.at[j - 1], at(j))
            for j in range(1, count)
        ]

    def hot_gather(axis):
        hot_wait()
        if axis == "z":
            got = hp[pl.ds(base_z, hrz), :]
            for j in range(1, nz):
                got = got + hz[j - 1]
            own_z = pl.multiple_of(base_c + base_z, 8)
            hsum[pl.ds(own_z, hrz), :] = got
            ref, peers = hsum.at[pl.ds(own_z, hrz)], [at_z(j) for j in range(1, nz)]
        elif axis == "y":
            ref = hsum.at[pl.ds(pl.multiple_of(base_c + base_y, 8), hry)]
            peers = [at_second(j) for j in range(1, ny)]
        elif axis == "x":
            ref = hsum.at[pl.ds(pl.multiple_of(base_c + base_x, 8), hrx)]
            peers = [at_first(j) for j in range(1, nx)]
        else:
            ref, peers = hsum.at[pl.ds(base_c, hot_rows)], [partner]
        todo["hot"] = [send(ref, ref, peer) for peer in peers]

    def numbers_on():
        every_mp(lambda p: ids_one(p).wait_recv())
        idmid[here_slot] = idsend[here_slot * n_dp : (here_slot + 1) * n_dp, :]
        for i in range(n_dp):
            idout[i] = jnp.concatenate([idmid[p, i : i + 1, :] for p in range(n_mp)], axis=0)
        for i in others:
            ids_two(i).start()

    band8 = LANES // deep

    def numbers_in():
        for i in others:
            ids_two(i).wait_recv()
        idfin[here_dp] = idout[here_dp]
        digits = idfin[...].reshape(devices, LANES).astype(BF16)
        at_lane, at_digit = iota((LANES, 2 * LANES), 1), iota((LANES, 2 * LANES), 0)
        want = (at_lane // LANES) * deep + at_lane % deep
        high = dot(digits, jnp.where(at_digit == want, 1.0, 0.0).astype(BF16))
        low = dot(digits, jnp.where(at_digit == want + cap, 1.0, 0.0).astype(BF16))
        numbers = high * 64.0 + low - 64.0
        keep = (iota(numbers.shape, 1) % LANES) // deep == iota(numbers.shape, 0) % band8
        numbers = jnp.where(keep, numbers, 0.0)
        numbers = jnp.sum(numbers.reshape(devices // band8, band8, 2 * LANES), axis=1)
        ids[...] = numbers.astype(I32)

    def forward(q):
        every_mp(lambda p: cold_one(q, p).wait_recv())
        for k in range(each):
            if q * each + k == here_dp:
                fin[q, k] = mid[q, :, k]
            else:
                cold_two(q, k).start()

    cold_half = cold.shape[0]
    per = each * n_mp * deep
    pieces = per // LANES
    step = 256

    def gather(g):
        for k in range(each):
            if g * each + k != here_dp:
                cold_two(g, k).wait_recv()
        eye = iota((LANES, LANES), 0) == iota((LANES, LANES), 1)
        ones = jnp.ones((LANES, LANES), BF16)
        for q in range(pieces):
            run = q % (n_mp // band8) * band8
            grads = fin[g, q // (n_mp // band8), run : run + band8].reshape(LANES, 2 * LANES)
            for k in range(2):
                number = ids[g * pieces + q : g * pieces + q + 1, k * LANES : (k + 1) * LANES]
                upper = jnp.where(number >= cold_half, 1.0, 0.0)
                column = dot(jnp.where(eye, upper, 0.0).astype(BF16), ones)
                split_columns(arhs, k * per + q * LANES, grads[:, k * LANES : (k + 1) * LANES], column > 0.5)

        def block(m, _):
            for q in range(pieces):
                for k in range(2):
                    number = ids[g * pieces + q : g * pieces + q + 1, k * LANES : (k + 1) * LANES]
                    number = jnp.where(number >= cold_half, number - cold_half, number)
                    at = k * per + q * LANES
                    alhs[:, at : at + LANES] = onehot(step, number - m * step)
            at = pl.ds(pl.multiple_of(m * step, 8), step)
            part = dot(alhs[...], arhs[...])
            if g == 0:
                cold[at, :] = part
            else:
                cold[at, :] = cold[at, :] + part
            return 0

        lax.fori_loop(0, cold_half // step, block, 0)

    for action, *given in PLAN:
        {
            "bucket": bucket_quarter, "cores": cores, "far": far, "near": near, "own": own, "join": join,
            "end": end, "join2": join2, "end2": end2, "along_z": along_z, "end_z": end_z, "weights": weights,
            "hot_product": hot_product, "hot_scatter": hot_scatter, "hot_gather": hot_gather, "hot_wait": hot_wait,
            "numbers_on": numbers_on, "numbers_in": numbers_in, "forward": forward, "gather": gather,
        }[action](*given)

    for copy in copies:
        copy.wait_send()
    every_mp(lambda p: ids_one(p).wait_send())
    for q in range(quarters):
        every_mp(lambda p: cold_one(q, p).wait_send())
    for i in others:
        ids_two(i).wait_send()
        cold_two(i // each, i % each).wait_send()


def update_kernel(
    wg_ref, hot_ref, cold_ref, w_ref, a_ref, ht_ref, ha_ref, ct_ref, ca_ref,
    nw_ref, na_ref, nh_ref, nha_ref, nc_ref, nca_ref,
):
    m, steps = pl.program_id(0), pl.num_programs(0)

    @pl.when(m == 0)
    def _():
        grad = wg_ref[...]
        accum = a_ref[...] + grad * grad
        na_ref[...] = accum
        nw_ref[...] = w_ref[...] - RATE * grad / jnp.sqrt(accum)

    parts = hot_ref.shape[0] // LANES
    for part in range(parts):
        at, line = slice(part * LANES, (part + 1) * LANES), pl.ds(m * parts + part, 1)
        nh_ref[at, :], nha_ref[line, :] = adagrad_block(ht_ref[at, :], ha_ref[line, :], hot_ref[at, :])
    parts = cold_ref.shape[0] // LANES
    for upper in range(2):
        for part in range(parts):
            at, line = slice(part * LANES, (part + 1) * LANES), pl.ds((upper * steps + m) * parts + part, 1)
            grad = cold_ref[at, upper * LANES : (upper + 1) * LANES]
            nc_ref[upper, at, :], nca_ref[line, :] = adagrad_block(ct_ref[upper, at, :], ca_ref[line, :], grad)


def shards(
    nx, ny, nz,
    pooled_in, out_grad, pooled_grad, hot_ids, cold_owner, cold_rows,
    mlp_weight, mlp_accum, hot_table, hot_accum, cold_table, cold_accum,
):
    n_dp, n_mp = nx * ny, nz * 2
    devices = n_dp * n_mp
    samples, features = hot_ids.shape
    hid = pooled_in.shape[1]
    hot = hot_table.shape[0]
    rows = cold_table.shape[0]
    lookups = samples * features
    cap = 2 * lookups // devices
    deep = cap // 2
    group_slots = 2 * (n_dp * (n_mp // 4) * deep)
    quarter = hid // 4
    chunk, tile = hid // nx, hid // (nx * ny)
    band = tile // nz
    half_hot = hot // 2
    hrx, hry, hrz = half_hot // nx, half_hot // (nx * ny), half_hot // (nx * ny * nz)
    pieces = 2 * SPLITS
    width = quarter // SPLITS
    n_copies = 4 + pieces * 6 * 2 + SPLITS * nz + 2 * (nx - 1 + ny - 1 + nz - 1)
    dma = pltpu.SemaphoreType.DMA
    weight_grad, hot_grad, cold_grad = pl.pallas_call(
        functools.partial(step_kernel, nx, ny, nz, SPLITS, cap, float(samples * devices) ** (-0.5)),
        out_shape=(
            jax.ShapeDtypeStruct(mlp_weight.shape, F32),
            jax.ShapeDtypeStruct(hot_table.shape, F32),
            jax.ShapeDtypeStruct((rows // 2, 2 * LANES), F32),
        ),
        in_specs=[VMEM] * 6,
        out_specs=(VMEM,) * 3,
        scratch_shapes=[
            pltpu.VMEM((samples, hid), BF16),
            pltpu.VMEM((samples, hid // 2), BF16),
            pltpu.VMEM((pieces, 4, chunk, width), F32),
            pltpu.VMEM((pieces, 6, chunk // 2, width), F32),
            pltpu.VMEM((pieces, 6, tile // 2, width), F32),
            pltpu.VMEM((SPLITS, tile, 2 * width), F32),
            pltpu.VMEM((SPLITS, nz - 1, band, 2 * width), F32),
            pltpu.VMEM((SPLITS, band, 2 * width), F32),
            pltpu.VMEM((SPLITS, band // 2, 2 * width), F32),
            pltpu.VMEM((lookups, 2 * LANES), BF16),
            pltpu.VMEM((features, samples), I32),
            pltpu.VMEM((half_hot, 2 * LANES), F32),
            pltpu.VMEM((half_hot, LANES), F32),
            pltpu.VMEM((nx - 1, hrx, LANES), F32),
            pltpu.VMEM((ny - 1, hry, LANES), F32),
            pltpu.VMEM((nz - 1, hrz, LANES), F32),
            pltpu.VMEM((features, samples), F32),
            pltpu.VMEM((features, samples), I32),
            pltpu.VMEM((lookups, 2 * LANES), BF16),
            pltpu.VMEM((samples, lookups), BF16),
            pltpu.VMEM((4, n_mp, n_dp // 4, deep, 2 * LANES), BF16),
            pltpu.VMEM((4, n_mp, n_dp // 4, deep, 2 * LANES), BF16),
            pltpu.VMEM((4, n_dp // 4, n_mp, deep, 2 * LANES), BF16),
            pltpu.VMEM((devices, LANES), F32),
            pltpu.VMEM((n_mp, n_dp, LANES), F32),
            pltpu.VMEM((n_dp, n_mp, LANES), F32),
            pltpu.VMEM((n_dp, n_mp, LANES), F32),
            pltpu.VMEM((devices * deep // LANES, 2 * LANES), I32),
            pltpu.VMEM((group_slots, 2 * LANES), BF16),
            pltpu.VMEM((256, group_slots), BF16),
            dma((n_copies,)), dma((n_copies,)),
            dma((4, n_mp)), dma((4, n_mp)),
            dma((4, n_dp // 4)), dma((4, n_dp // 4)),
            dma((n_mp,)), dma((n_mp,)),
            dma((n_dp,)), dma((n_dp,)),
        ],
        compiler_params=pltpu.CompilerParams(
            vmem_limit_bytes=58 << 20, collective_id=0, has_side_effects=True
        ),
        name="step",
    )(
        pooled_in, out_grad, pooled_grad, hot_ids.T, cold_owner.T, cold_rows.T
    )

    steps = STEPS
    whole = lambda *shape: pl.BlockSpec(shape, lambda m: (0,) * len(shape))
    hot_block = pl.BlockSpec((hot // steps, LANES), lambda m: (m, 0))
    cold_block = pl.BlockSpec((2, rows // 2 // steps, LANES), lambda m: (0, m, 0))
    weight = whole(*mlp_weight.shape)
    hot_line, cold_line = whole(hot // LANES, LANES), whole(rows // LANES, LANES)
    new_weight, new_mlp_accum, new_hot, new_hot_accum, new_cold, new_cold_accum = pl.pallas_call(
        update_kernel,
        grid=(steps,),
        out_shape=(
            jax.ShapeDtypeStruct(mlp_weight.shape, F32),
            jax.ShapeDtypeStruct(mlp_accum.shape, F32),
            jax.ShapeDtypeStruct(hot_table.shape, F32),
            jax.ShapeDtypeStruct((hot // LANES, LANES), F32),
            jax.ShapeDtypeStruct((2, rows // 2, LANES), F32),
            jax.ShapeDtypeStruct((rows // LANES, LANES), F32),
        ),
        in_specs=[
            weight, hot_block, pl.BlockSpec((rows // 2 // steps, 2 * LANES), lambda m: (m, 0)),
            weight, weight, hot_block, hot_line, cold_block, cold_line,
        ],
        out_specs=(weight, weight, hot_block, hot_line, cold_block, cold_line),
        name="update",
    )(
        weight_grad, hot_grad, cold_grad, mlp_weight, mlp_accum,
        hot_table, hot_accum.reshape(hot // LANES, LANES),
        cold_table.reshape(2, rows // 2, LANES), cold_accum.reshape(rows // LANES, LANES),
    )
    return (
        new_weight,
        new_mlp_accum,
        new_hot,
        new_hot_accum.reshape(hot),
        new_cold.reshape(rows, LANES),
        new_cold_accum.reshape(rows),
    )


def solution(mesh):
    split = P(("dp", "mp"), None)
    nx = ny = 4
    nz = mesh.shape["mp"] // 2
    return jax.shard_map(
        functools.partial(shards, nx, ny, nz),
        mesh=mesh,
        in_specs=(split,) * 8 + (P(), P(), split, P(("dp", "mp"))),
        out_specs=(split, split, P(), P(), split, P(("dp", "mp"))),
        check_vma=False,
    )
```
